32 devices in a mesh: dp: 8 (over z, y), modes: 4 (over x, core).
Axes of the slice: x: 2, y: 2, z: 4, core: 2. Of those that a mesh axis runs over, the one named last changes fastest.
Arguments:
- grids_big: bfloat16 [16, 128, 24576], P('dp', 'modes'), may hold values from -6 to 6
- grids_small: bfloat16 [32, 64, 12288], P('dp', 'modes'), may hold values from -6 to 6
- counts_big: int32 [8], P('dp'), may hold values from 1 to 2, as said below
- counts_small: int32 [8], P('dp'), may hold values from 1 to 4, as said below
- mode_table: int32 [16], replicated, may hold values from 0 to 15, each once
- spec_one: bfloat16 [16, 16, 4, 48, 48], P('modes'), may hold values from -1.25 to 1.25
- point_one: bfloat16 [4, 48, 48], replicated, may hold values from -0.4375 to 0.4375
- bias_one: float32 [192], replicated, may hold values from -1.5 to 1.5
- spec_two: bfloat16 [16, 16, 4, 48, 48], P('modes'), may hold values from -1.25 to 1.25
- point_two: bfloat16 [4, 48, 48], replicated, may hold values from -0.4375 to 0.4375
- bias_two: float32 [192], replicated, may hold values from -1.5 to 1.5
- cot_big: bfloat16 [16, 128, 24576], P('dp', 'modes'), may hold values from -6 to 6
- cot_small: bfloat16 [32, 64, 12288], P('dp', 'modes'), may hold values from -6 to 6
Outputs:
- out_big: bfloat16 [16, 128, 24576], P('dp', 'modes')
- out_small: bfloat16 [32, 64, 12288], P('dp', 'modes')
- grad_big: bfloat16 [16, 128, 24576], P('dp', 'modes')
- grad_small: bfloat16 [32, 64, 12288], P('dp', 'modes')
- spec_grad_one: float32 [16, 147456], P('modes', 'dp')
- point_grad_one: float32 [4, 48, 48], replicated
- bias_grad_one: float32 [192], replicated
- spec_grad_two: float32 [16, 147456], P('modes', 'dp')
- point_grad_two: float32 [4, 48, 48], replicated
- bias_grad_two: float32 [192], replicated
The draws below stay inside these ranges and needn't reach their ends.
Inputs may be any that keep to these rules, and one draw needn't show every extreme that they name: `counts_big`: slots 0 to count - 1 of an index of dp are live; some index holds 2. `counts_small`: slots 0 to count - 1 of an index of dp are live; some index holds 4. `mode_table`: each frequency index appears once.
All inputs are finite; a program needn't handle non-finite values.
Results may differ from the reference program's by a relative error of at most 0.029.
Values may be sent and summed in bfloat16 or wider, within the bound.
A program may use at most 384 MiB of HBM per device.

```python
import math
import jax
import jax.numpy as jnp
import numpy as np
from jax import lax

C = 48
KX = 16
KY = 16
HB = 128
WB = 128
HS = 64
WS = 64
SLOTS_BIG = 2
SLOTS_SMALL = 4
GROUPS = 8
SAMPLES_BIG = 16
SAMPLES_SMALL = 32


def draw_counts_big(key, part):
    key = jax.random.fold_in(key, 11)
    first_key, second_key = jax.random.split(key)
    counts = jax.random.randint(first_key, (GROUPS,), 1, SLOTS_BIG + 1)
    chosen = jax.random.randint(second_key, (), 0, GROUPS)
    return counts.at[chosen].set(SLOTS_BIG).astype(jnp.int32)


def draw_counts_small(key, part):
    key = jax.random.fold_in(key, 23)
    first_key, second_key = jax.random.split(key)
    counts = jax.random.randint(first_key, (GROUPS,), 1, SLOTS_SMALL + 1)
    chosen = jax.random.randint(second_key, (), 0, GROUPS)
    return counts.at[chosen].set(SLOTS_SMALL).astype(jnp.int32)


def block_scale(own_key, shape, cuts, least, largest):
    gain, own = 1.0, jax.random.fold_in(own_key, 6)
    for axis_at, shards_of in cuts:
        draws = jnp.exp(jax.random.uniform(jax.random.fold_in(own, axis_at), (shards_of,), jnp.float32, least / len(cuts), largest / len(cuts)))
        gain = gain * jnp.repeat(draws, shape[axis_at] // shards_of).reshape([-1 if axis == axis_at else 1 for axis in range(len(shape))])
    return gain


def centred(key, extent, scale, most, shards=(), held_as=jnp.bfloat16):
    values = jax.random.normal(key, extent, jnp.float32) * scale
    if len(shards) > 0:
        values = block_scale(key, extent, shards, -0.22, 0.18) * values
    return jnp.clip(values, min=-most, max=most).astype(held_as)


def setup_inputs(seed: int = 0) -> dict:
    key_list = jax.random.split(jax.random.key(seed), 14)
    grids_big = centred(key_list[0], (SAMPLES_BIG, HB, WB * 4 * C), 1.0, 6.0, ((0, 8), (1, 4)))
    grids_small = centred(key_list[1], (SAMPLES_SMALL, HS, WS * 4 * C), 1.0, 6.0, ((0, 8), (1, 4)))
    counts_big = draw_counts_big(jax.random.fold_in(key_list[13], 71), 0)
    counts_small = draw_counts_small(jax.random.fold_in(key_list[13], 71), 0)
    mode_table = jax.random.permutation(key_list[4], KX).astype(jnp.int32)
    spec_one = centred(key_list[5], (KX, KY, 4, C, C), (C // 2) ** -0.5, 1.25, ((0, 4),))
    point_one = centred(key_list[6], (4, C, C), (4 * C) ** -0.5, 0.4375)
    bias_one = centred(key_list[7], (4 * C,), 0.3, 1.5, (), jnp.float32)
    spec_two = centred(key_list[8], (KX, KY, 4, C, C), (C // 2) ** -0.5, 1.25, ((0, 4),))
    point_two = centred(key_list[9], (4, C, C), (4 * C) ** -0.5, 0.4375)
    bias_two = centred(key_list[10], (4 * C,), 0.3, 1.5, (), jnp.float32)
    cot_big = centred(key_list[11], (SAMPLES_BIG, HB, WB * 4 * C), 1.0, 6.0, ((0, 8), (1, 4)))
    cot_small = centred(key_list[12], (SAMPLES_SMALL, HS, WS * 4 * C), 1.0, 6.0, ((0, 8), (1, 4)))
    return {"grids_big": grids_big, "grids_small": grids_small, "counts_big": counts_big, "counts_small": counts_small, "mode_table": mode_table, "spec_one": spec_one, "point_one": point_one, "bias_one": bias_one, "spec_two": spec_two, "point_two": point_two, "bias_two": bias_two, "cot_big": cot_big, "cot_small": cot_small}


@jax.custom_vjp
def low(v):
    return lax.optimization_barrier(v.astype(jnp.bfloat16)).astype(jnp.float32)

@jax.custom_vjp
def low_back(v):
    return v

def low_keep(v):
    return (low(v), None)

def low_pass(kept, grad):
    return (grad,)

def back_keep(v):
    return (v, None)

def back_low(kept, grad):
    return (low(grad),)
low.defvjp(low_keep, low_pass)
low_back.defvjp(back_keep, back_low)
HIGH = lax.Precision.HIGHEST
SELECT = np.array([[0, 1, 2, 3], [1, 0, 3, 2], [2, 3, 0, 1], [3, 2, 1, 0]])
SIGNS = np.array([[1.0, 1.0, 1.0, -1.0], [1.0, 1.0, 1.0, -1.0], [1.0, -1.0, 1.0, 1.0], [1.0, -1.0, 1.0, 1.0]])

def blade_matrix(weight):
    count = weight.shape[-1]
    leading = weight.shape[:-3]
    blocks = jnp.stack([weight[..., int(SELECT[out_blade, in_blade]), :, :] * float(SIGNS[out_blade, in_blade]) for out_blade in range(4) for in_blade in range(4)], axis=-3)
    blocks = blocks.reshape(leading + (4, 4, count, count))
    blocks = jnp.swapaxes(blocks, -3, -2)
    return blocks.reshape(leading + (4 * count, 4 * count))

def column_table(width):
    position = jnp.arange(width, dtype=jnp.int32)[:, None]
    frequency = jnp.arange(KY, dtype=jnp.int32)[None, :]
    phase = (position * frequency % width).astype(jnp.float32) * (2.0 * math.pi / width)
    return jnp.stack([jnp.cos(phase), -jnp.sin(phase)], axis=-1).astype(jnp.bfloat16)

def row_table(height, mode_table, first_row, count):
    frequency = jnp.where(mode_table < KX // 2, mode_table, mode_table - KX)
    position = first_row + jnp.arange(count, dtype=jnp.int32)
    phase = (frequency[:, None] * position[None, :] % height).astype(jnp.float32) * (2.0 * math.pi / height)
    return jnp.stack([jnp.cos(phase), jnp.sin(phase)], axis=1).astype(jnp.bfloat16)

def inverse_table(column, height, width):
    factor = jnp.where(jnp.arange(KY) == 0, 1.0, 2.0) / (height * width)
    scaled = column.astype(jnp.float32) * factor[None, :, None]
    return jnp.transpose(scaled, (1, 2, 0)).astype(jnp.bfloat16)

def grid_set(height, width, mode_table):
    column = column_table(width)
    rowwise = row_table(height, mode_table, 0, height)
    inverse = inverse_table(column, height, width)
    return (column.astype(jnp.float32), rowwise.astype(jnp.float32), inverse.astype(jnp.float32))

def layer(state, spectral, pointwise, offset, tables):
    column, rowwise, inverse = tables
    active = low(state)
    columns = low(low_back(jnp.einsum('hwc,wkr->hkrc', active, column, precision=HIGH)))
    cosine_part = jnp.einsum('mh,hkrc->mkrc', rowwise[:, 0], columns, precision=HIGH)
    sine_part = jnp.einsum('mh,hkrc->mkrc', rowwise[:, 1], columns, precision=HIGH)
    spectrum = jnp.stack([cosine_part[:, :, 0] + sine_part[:, :, 1], cosine_part[:, :, 1] - sine_part[:, :, 0]], axis=2)
    spectrum = low(low_back(spectrum))
    answer = low(low_back(jnp.einsum('mkoi,mkri->mkro', spectral, spectrum, precision=HIGH)))
    cosine_part = jnp.einsum('mh,mkrc->hkrc', rowwise[:, 0], answer, precision=HIGH)
    sine_part = jnp.einsum('mh,mkrc->hkrc', rowwise[:, 1], answer, precision=HIGH)
    field = jnp.stack([cosine_part[:, :, 0] - sine_part[:, :, 1], cosine_part[:, :, 1] + sine_part[:, :, 0]], axis=2)
    field = low(low_back(field))
    spatial = jnp.einsum('hkrc,krw->hwc', field, inverse, precision=HIGH)
    linear = jnp.einsum('hwi,oi->hwo', active, pointwise, precision=HIGH)
    before = low_back(spatial + linear + offset)
    return state + jax.nn.gelu(before, approximate=False)

def reference(grids_big, grids_small, counts_big, counts_small, mode_table, spec_one, point_one, bias_one, spec_two, point_two, bias_two, cot_big, cot_small):
    tables_big = grid_set(HB, WB, mode_table)
    tables_small = grid_set(HS, WS, mode_table)
    live_big = (jnp.arange(SLOTS_BIG, dtype=jnp.int32)[None, :] < counts_big[:, None]).reshape(-1)
    live_big = live_big.astype(jnp.float32)[:, None, None, None]
    live_small = (jnp.arange(SLOTS_SMALL, dtype=jnp.int32)[None, :] < counts_small[:, None]).reshape(-1)
    live_small = live_small.astype(jnp.float32)[:, None, None, None]
    shape_big = (SAMPLES_BIG, HB, WB, 4 * C)
    shape_small = (SAMPLES_SMALL, HS, WS, 4 * C)

    def forward(big_grids, small_grids, spec_first, point_first, bias_first, spec_second, point_second, bias_second):
        matrices = (blade_matrix(spec_first), blade_matrix(point_first), bias_first, blade_matrix(spec_second), blade_matrix(point_second), bias_second)

        def run(grids, tables):

            def both_layers(state):
                state = layer(state, matrices[0], matrices[1], matrices[2], tables)
                return layer(state, matrices[3], matrices[4], matrices[5], tables)
            return lax.map(jax.checkpoint(both_layers), grids)
        return (run(big_grids, tables_big) * live_big, run(small_grids, tables_small) * live_small)
    primal = (grids_big.astype(jnp.float32).reshape(shape_big), grids_small.astype(jnp.float32).reshape(shape_small), spec_one.astype(jnp.float32), point_one.astype(jnp.float32), bias_one.astype(jnp.float32), spec_two.astype(jnp.float32), point_two.astype(jnp.float32), bias_two.astype(jnp.float32))
    outputs, pullback = jax.vjp(forward, *primal)
    grads = pullback((cot_big.astype(jnp.float32).reshape(shape_big), cot_small.astype(jnp.float32).reshape(shape_small)))
    flat_big = (SAMPLES_BIG, HB, WB * 4 * C)
    flat_small = (SAMPLES_SMALL, HS, WS * 4 * C)
    return (outputs[0].reshape(flat_big).astype(jnp.bfloat16), outputs[1].reshape(flat_small).astype(jnp.bfloat16), grads[0].reshape(flat_big).astype(jnp.bfloat16), grads[1].reshape(flat_small).astype(jnp.bfloat16), grads[2].reshape(KX, -1), grads[3], grads[4], grads[5].reshape(KX, -1), grads[6], grads[7])
```

```python
import math

import jax
import jax.numpy as jnp
import numpy as np
from jax import lax
from jax.experimental import pallas as pl
from jax.experimental.pallas import tpu as pltpu
from jax.sharding import PartitionSpec as P

BF, F32 = jnp.bfloat16, jnp.float32
KX = 16
KY = 16
C = 192
CH = 48
K = 32
PAIR = 2 * C
LIMIT = 60 * 2**20
SELECT = np.array([[0, 1, 2, 3], [1, 0, 3, 2], [2, 3, 0, 1], [3, 2, 1, 0]])
SIGNS = np.array(
    [[1.0, 1.0, 1.0, -1.0], [1.0, 1.0, 1.0, -1.0], [1.0, -1.0, 1.0, 1.0], [1.0, -1.0, 1.0, 1.0]]
)


def dot(a, b):
    return jnp.dot(a, b, preferred_element_type=F32)


def dot_nt(a, b):
    return lax.dot_general(a, b, (((1,), (1,)), ((), ())), preferred_element_type=F32)


def dot_tn(a, b):
    return lax.dot_general(a, b, (((0,), (0,)), ((), ())), preferred_element_type=F32)


def to_bf(values):
    return np.asarray(values, np.float32).astype(jnp.bfloat16)


def column_tables(height, width):
    position = np.arange(width)[:, None]
    frequency = np.arange(KY)[None, :]
    phase = ((position * frequency) % width).astype(np.float32) * np.float32(2.0 * math.pi / width)
    col = to_bf(np.stack([np.cos(phase), -np.sin(phase)], -1)).astype(np.float32)
    factor = np.where(np.arange(KY) == 0, 1.0, 2.0) / (height * width)
    inv = to_bf(col * factor[None, :, None].astype(np.float32)).astype(np.float32)
    half = width // 2

    def analysis_form(table):
        return to_bf(table.reshape(half, 2, KY, 2).transpose(3, 2, 1, 0).reshape(K, width))

    def synthesis_form(table):
        return to_bf(table.reshape(half, 2, KY, 2).transpose(0, 1, 3, 2).reshape(half, 2 * K))

    return analysis_form(col), synthesis_form(inv), analysis_form(inv), synthesis_form(col)


def blade_tables():
    eye = np.eye(CH)
    spread = np.zeros((2, 4, 256, C))
    gather = np.zeros((2, 4, C, PAIR))
    copies = np.zeros((2, 4, 256, C))
    unfold = np.zeros((2, 4, C, PAIR))
    for parity in range(2):
        for p in range(4):
            for b in range(4):
                q = int(np.where(SELECT[p] == b)[0][0])
                sign = SIGNS[p, q]
                row = parity * 64 + q * CH
                spread[parity, p, row : row + CH, b * CH : (b + 1) * CH] = sign * eye
                lane = parity * C + q * CH
                unfold[parity, p, b * CH : (b + 1) * CH, lane : lane + CH] = sign * eye
                lane = parity * C + p * CH
                gather[parity, p, b * CH : (b + 1) * CH, lane : lane + CH] = eye
                row = parity * 64 + p * CH
                copies[parity, p, row : row + CH, b * CH : (b + 1) * CH] = eye
    return to_bf(spread), to_bf(gather), to_bf(copies), to_bf(unfold)


def analysis(block, table):
    stacked = jnp.concatenate([block[:, :C], block[:, C:]], axis=0)
    return dot(table, stacked)


def put_field(field, n, value):
    field[0, pl.ds(n * K, K), :] = value[:, :128]
    field[1, pl.ds(n * K, K), 0:64] = value[:, 128:]


def get_rows(field, k, count):
    low = field[0, pl.ds(k, count, stride=K), :]
    high = field[1, pl.ds(k, count, stride=K), :]
    return jnp.concatenate([low, high[:, :64]], axis=1).astype(BF)


def rows_forward(field, matrix, ky2, count):
    parts = []
    for parity in range(2):
        ky = ky2 * 2 + parity
        parts.append(
            jnp.concatenate([get_rows(field, ky, count), get_rows(field, KY + ky, count)], axis=0)
        )
    return dot(matrix, jnp.concatenate(parts, axis=1))


def rows_inverse(field, matrix_t, spectrum, ky2, count):
    for parity in range(2):
        value = dot(matrix_t, spectrum[:, parity * C : (parity + 1) * C])
        ky = ky2 * 2 + parity
        for part in range(2):
            piece = value[part * count : (part + 1) * count]
            field[0, pl.ds(part * KY + ky, count, stride=K), :] = piece[:, :128]
            field[1, pl.ds(part * KY + ky, count, stride=K), :] = jnp.concatenate(
                [piece[:, 128:], jnp.zeros((count, 64), F32)], axis=1
            )


def synthesis(field, n, table):
    value = jnp.concatenate(
        [field[0, pl.ds(n * K, K), :], field[1, pl.ds(n * K, K), 0:64]], axis=1
    ).astype(BF)
    zero = jnp.zeros((K, C), BF)
    both = jnp.concatenate(
        [jnp.concatenate([value, zero], axis=1), jnp.concatenate([zero, value], axis=1)], axis=0
    )
    return dot(table, both)


def pointwise(block, first, second):
    left = dot(block[:, :256], first)
    right = dot(block[:, 128:], second)
    return jnp.concatenate(
        [left[:, :128], left[:, 128:] + right[:, :128], right[:, 128:]], axis=1
    )


def gelu_and_slope(value):
    cdf = 0.5 + 0.5 * lax.erf(value * (1.0 / math.sqrt(2.0)))
    bell = jnp.exp(-0.5 * value * value)
    return value * cdf, cdf + value * bell * (1.0 / math.sqrt(2.0 * math.pi))


def mode_mask(rows, group_rows):
    row = lax.broadcasted_iota(jnp.int32, (rows, C), 0)
    lane = lax.broadcasted_iota(jnp.int32, (rows, C), 1)
    return (row % group_rows) // (group_rows // 4) == lane // CH


class Group:
    def __init__(self, slots, rows, width, parts):
        self.slots, self.rows, self.width = slots, rows, width
        self.count = slots * rows
        self.half = width // 2
        self.pairs = self.count * self.half
        self.block = 256 // self.half
        self.own = 4 * slots * 2
        self.full = parts * self.own


def loop(count, body, unroll=1):
    def step(i, carry):
        body(i)
        return carry

    lax.fori_loop(0, count, step, 0, unroll=unroll)


def call(kernel, outs, scratch=()):
    return pl.pallas_call(
        kernel,
        out_shape=outs,
        scratch_shapes=list(scratch),
        compiler_params=pltpu.CompilerParams(vmem_limit_bytes=LIMIT),
    )


def struct(shape, dtype=BF):
    return jax.ShapeDtypeStruct(shape, dtype)


def field_scratch(group):
    return pltpu.VMEM((2, group.count * K, 128), F32)


STEP = 16


def pack_kernel(count_ref, x_ref, o_ref, scratch, *, slots, masked):
    rows = x_ref.shape[0]
    per = rows // slots
    if masked:
        index = lax.broadcasted_iota(jnp.int32, (rows, PAIR), 0) // per
        live = (index < count_ref[0]).astype(F32)
    for j in range(STEP):
        slab = x_ref[:, j * PAIR : (j + 1) * PAIR].astype(F32)
        if masked:
            slab = slab * live
        for t in range(3):
            scratch[t, pl.ds(j * rows, rows), :] = slab[:, t * 128 : (t + 1) * 128]
    for n in range(rows):
        o_ref[n] = jnp.concatenate(
            [scratch[t, pl.ds(n, STEP, stride=rows), :] for t in range(3)], axis=1
        ).astype(BF)


def pack(x, counts, group, masked):
    x = x.reshape(group.count, group.width * C)
    out = pl.pallas_call(
        lambda *refs: pack_kernel(*refs, slots=group.slots, masked=masked),
        grid=(group.half // STEP,),
        in_specs=[
            pl.BlockSpec(memory_space=pltpu.SMEM),
            pl.BlockSpec((group.count, STEP * PAIR), lambda i: (0, i)),
        ],
        out_specs=pl.BlockSpec((group.count, STEP, PAIR), lambda i: (0, i, 0)),
        out_shape=struct((group.count, group.half, PAIR)),
        scratch_shapes=[pltpu.VMEM((3, STEP * group.count, 128), F32)],
        compiler_params=pltpu.CompilerParams(vmem_limit_bytes=LIMIT),
    )(counts, x)
    return out.reshape(group.pairs, PAIR)


def unpack_kernel(count_ref, x_ref, o_ref, scratch, *, slots, masked):
    rows = x_ref.shape[0]
    per = rows // slots
    for n in range(rows):
        value = x_ref[n].astype(F32)
        for t in range(3):
            scratch[t, pl.ds(n, STEP, stride=rows), :] = value[:, t * 128 : (t + 1) * 128]
    if masked:
        index = lax.broadcasted_iota(jnp.int32, (rows, PAIR), 0) // per
        live = (index < count_ref[0]).astype(F32)
    for j in range(STEP):
        slab = jnp.concatenate([scratch[t, pl.ds(j * rows, rows), :] for t in range(3)], axis=1)
        if masked:
            slab = slab * live
        o_ref[:, j * PAIR : (j + 1) * PAIR] = slab.astype(BF)


def unpack(x, counts, group, masked):
    out = pl.pallas_call(
        lambda *refs: unpack_kernel(*refs, slots=group.slots, masked=masked),
        grid=(group.half // STEP,),
        in_specs=[
            pl.BlockSpec(memory_space=pltpu.SMEM),
            pl.BlockSpec((group.count, STEP, PAIR), lambda i: (0, i, 0)),
        ],
        out_specs=pl.BlockSpec((group.count, STEP * PAIR), lambda i: (0, i)),
        out_shape=struct((group.count, group.width * C)),
        scratch_shapes=[pltpu.VMEM((3, STEP * group.count, 128), F32)],
        compiler_params=pltpu.CompilerParams(vmem_limit_bytes=LIMIT),
    )(counts, x.reshape(group.count, group.half, PAIR))
    return out.reshape(group.slots, group.rows, group.width * C)


def analyse_rows(source, table, field, group, index):
    t = table[...]
    for q in range(group.block):
        n = index * group.block + q
        put_field(field, n, analysis(source[pl.ds(n * group.half, group.half), :], t))


def send_rows(field, matrix, out, group):
    def body(ky2):
        value = rows_forward(field, matrix[...], ky2, group.count).astype(BF)
        for owner in range(4):
            out[owner, ky2] = value[owner * group.own : (owner + 1) * group.own]

    loop(KY // 2, body, unroll=4)


def receive_rows(field, matrix_t, spectrum, group):
    def body(ky2):
        value = jnp.concatenate([spectrum[owner, ky2] for owner in range(4)], axis=0)
        rows_inverse(field, matrix_t[...], value, ky2, group.count)

    loop(KY // 2, body, unroll=4)


def first_kernel(a, table, matrix, out, field, *, group):
    loop(group.count // group.block, lambda i: analyse_rows(a, table, field, group, i), unroll=2)
    send_rows(field, matrix, out, group)


def synth_block(field, table, group, index):
    return jnp.concatenate(
        [synthesis(field, index * group.block + q, table[...]) for q in range(group.block)], axis=0
    )


def middle_kernel(y, a, first, second, bias, syn, ana, matrix, matrix_t, out, slope, send, field, *, group):
    receive_rows(field, matrix_t, y, group)

    def body(i):
        rows = pl.ds(pl.multiple_of(i * 256, 256), 256)
        x = a[rows, :]
        s = synth_block(field, syn, group, i) + pointwise(x, first[...], second[...]) + bias[...]
        gelu, sl = gelu_and_slope(s)
        out[rows, :] = (x.astype(F32) + gelu).astype(BF)
        slope[rows, :] = sl.astype(BF)
        analyse_rows(out, ana, field, group, i)

    loop(group.count // group.block, body, unroll=2)
    send_rows(field, matrix, send, group)


def point_sums(ds, a, sums, bias_sum):
    sums[0] += dot_tn(ds[:, :256], a[:, :256])
    sums[1] += dot_tn(ds[:, 128:], a[:, 128:])
    bias_sum[...] += jnp.sum(ds.astype(F32).reshape(32, 8, PAIR), axis=0)


def turn_kernel(y, a, g, first, second, bias, syn, ana, matrix, matrix_t, out, ds, send, sums, bias_sum, field, *, group):
    receive_rows(field, matrix_t, y, group)
    sums[...] = jnp.zeros_like(sums)
    bias_sum[...] = jnp.zeros_like(bias_sum)

    def body(i):
        rows = pl.ds(pl.multiple_of(i * 256, 256), 256)
        x = a[rows, :]
        s = synth_block(field, syn, group, i) + pointwise(x, first[...], second[...]) + bias[...]
        gelu, sl = gelu_and_slope(s)
        out[rows, :] = (x.astype(F32) + gelu).astype(BF)
        d = (g[rows, :].astype(F32) * sl).astype(BF)
        ds[rows, :] = d
        point_sums(d, x, sums, bias_sum)
        analyse_rows(ds, ana, field, group, i)

    loop(group.count // group.block, body, unroll=1)
    send_rows(field, matrix, send, group)


def back_kernel(y, d2, g, slope, a, first, second, syn, ana, matrix, matrix_t, out, ds, send, sums, bias_sum, field, *, group):
    receive_rows(field, matrix_t, y, group)
    sums[...] = jnp.zeros_like(sums)
    bias_sum[...] = jnp.zeros_like(bias_sum)

    def body(i):
        rows = pl.ds(pl.multiple_of(i * 256, 256), 256)
        g1 = (
            synth_block(field, syn, group, i)
            + pointwise(d2[rows, :], first[...], second[...])
            + g[rows, :].astype(F32)
        )
        out[rows, :] = g1.astype(BF)
        d = (g1 * slope[rows, :].astype(F32)).astype(BF)
        ds[rows, :] = d
        point_sums(d, a[rows, :], sums, bias_sum)
        analyse_rows(ds, ana, field, group, i)

    loop(group.count // group.block, body, unroll=1)
    send_rows(field, matrix, send, group)


def last_kernel(y, d, g, first, second, syn, matrix_t, out, field, *, group):
    receive_rows(field, matrix_t, y, group)

    def body(i):
        rows = pl.ds(pl.multiple_of(i * 256, 256), 256)
        value = (
            synth_block(field, syn, group, i)
            + pointwise(d[rows, :], first[...], second[...])
            + g[rows, :].astype(F32)
        )
        out[rows, :] = value.astype(BF)

    loop(group.count // group.block, body, unroll=2)


def build_weights(raw, w2):
    def body(ky):
        parts = [
            jnp.concatenate([raw[m, ky, b] for m in range(4)], axis=0) for b in range(4)
        ]
        w2[ky] = jnp.concatenate(parts, axis=1)

    loop(KY, body, unroll=2)


def spread_rows(x, table, out, group, masked):
    rows = 8 * group.own
    value = x[...].reshape(rows, PAIR)
    mask = mode_mask(rows, group.own) if masked else None
    for parity in range(2):
        part = value[:, parity * 128 : parity * 128 + 256]
        for p in range(4):
            result = dot(part, table[parity, p])
            if masked:
                result = jnp.where(mask, result, 0.0)
            out[parity, p] = result.astype(BF)


def fold_rows(parts, table, out, group):
    total = None
    for parity in range(2):
        for p in range(4):
            term = dot(parts[parity, p], table[parity, p])
            total = term if total is None else total + term
    out[...] = total.astype(BF).reshape(8, group.own, PAIR)


def ky_rows(parts, parity, ky2, group):
    rows = pl.ds(pl.multiple_of(ky2 * group.own, group.own), group.own)
    return jnp.concatenate([parts[parity, p, rows, :] for p in range(4)], axis=0)


def set_ky_rows(parts, parity, ky2, group, value):
    rows = pl.ds(pl.multiple_of(ky2 * group.own, group.own), group.own)
    for p in range(4):
        parts[parity, p, rows, :] = value[p * group.own : (p + 1) * group.own]


def spectral_kernel(xb, xs, raw, spread, gather, yb, ys, w2, lb, ls, zb, zs, *, groups):
    build_weights(raw, w2)
    sets = list(zip(groups, (xb, xs), (lb, ls), (zb, zs), (yb, ys)))
    for group, x, l, z, y in sets:
        spread_rows(x, spread, l, group, False)

    def body(ky2):
        for parity in range(2):
            weight = w2[ky2 * 2 + parity]
            for group, x, l, z, y in sets:
                value = dot_nt(ky_rows(l, parity, ky2, group), weight)
                value = jnp.where(mode_mask(4 * group.own, group.own), value, 0.0).astype(BF)
                set_ky_rows(z, parity, ky2, group, value)

    loop(KY // 2, body, unroll=2)
    for group, x, l, z, y in sets:
        fold_rows(z, gather, y, group)


def spectral_back_kernel(db, ds, xb, xs, raw, spread, copies, unfold, yb, ys, dw, w2, lb, ls, ab, as_, zb, zs, *, groups):
    build_weights(raw, w2)
    sets = list(zip(groups, (xb, xs), (db, ds), (lb, ls), (ab, as_), (zb, zs), (yb, ys)))
    for group, x, d, l, a, z, y in sets:
        spread_rows(x, spread, l, group, False)
        spread_rows(d, copies, a, group, True)

    def body(ky2):
        grads = []
        for parity in range(2):
            weight = w2[ky2 * 2 + parity]
            lefts, rights = [], []
            for group, x, d, l, a, z, y in sets:
                left = ky_rows(a, parity, ky2, group)
                set_ky_rows(z, parity, ky2, group, dot(left, weight).astype(BF))
                lefts.append(left)
                rights.append(ky_rows(l, parity, ky2, group))
            grads.append(dot_tn(jnp.concatenate(lefts, axis=0), jnp.concatenate(rights, axis=0)))
        dw[ky2] = jnp.concatenate(grads, axis=1)

    loop(KY // 2, body, unroll=2)
    for group, x, d, l, a, z, y in sets:
        fold_rows(z, unfold, y, group)


def blade_matrix(weight):
    rows = [
        jnp.concatenate(
            [weight[int(SELECT[p, q])] * float(SIGNS[p, q]) for q in range(4)], axis=1
        )
        for p in range(4)
    ]
    return jnp.concatenate(rows, axis=0)


def pair_matrices(matrix):
    both = jnp.pad(matrix, ((0, C), (0, C))) + jnp.pad(matrix, ((C, 0), (C, 0)))
    second = both[128:, 128:]
    corner = np.ones((256, 256), np.float32)
    corner[:128, :128] = 0.0
    return both[:256, :256], second * corner.astype(second.dtype)


def row_matrix(mode_table, group, place, parts):
    height = group.rows * parts
    frequency = np.arange(KX)
    frequency = np.where(frequency < KX // 2, frequency, frequency - KX)
    phase = (frequency[:, None] * np.arange(height)[None, :]) % height
    phase = phase.astype(np.float32) * np.float32(2.0 * math.pi / height)
    table = jnp.asarray(np.stack([np.cos(phase), np.sin(phase)], 1).astype(np.float32))
    table = lax.dynamic_slice_in_dim(table, place * group.rows, group.rows, axis=2)[mode_table]
    cosine, sine = table[:, 0], table[:, 1]
    both = jnp.stack([jnp.stack([cosine, sine], 1), jnp.stack([-sine, cosine], 1)], 1)
    eye = jnp.eye(group.slots, dtype=F32)
    full = both[:, None, :, :, None, :] * eye[None, :, None, None, :, None]
    return full.reshape(KX * group.slots * 2, 2 * group.count).astype(BF)


def point_gradient(sums):
    total = sums[0][:C, :C] + sums[1][64:, 64:]
    blocks = total.reshape(4, CH, 4, CH)
    grads = []
    for b in range(4):
        grads.append(
            sum(
                float(SIGNS[p, q]) * blocks[p, :, q, :]
                for p in range(4)
                for q in range(4)
                if SELECT[p, q] == b
            )
        )
    return jnp.stack(grads)


def local(
    grids_big,
    grids_small,
    counts_big,
    counts_small,
    mode_table,
    spec_one,
    point_one,
    bias_one,
    spec_two,
    point_two,
    bias_two,
    cot_big,
    cot_small,
):
    parts = lax.axis_size("modes")
    place = lax.axis_index("modes")
    groups = [
        Group(g.shape[0], g.shape[1], g.shape[2] // C, parts) for g in (grids_big, grids_small)
    ]
    counts = (counts_big, counts_small)
    state = [pack(x, c, g, False) for x, c, g in zip((grids_big, grids_small), counts, groups)]
    grad = [pack(x, c, g, True) for x, c, g in zip((cot_big, cot_small), counts, groups)]
    tables = [
        [jnp.asarray(t) for t in column_tables(g.rows * parts, g.width)] for g in groups
    ]
    matrices = [row_matrix(mode_table, g, place, parts) for g in groups]
    matrices_t = [m.T for m in matrices]
    spread, gather, copies, unfold = [jnp.asarray(t) for t in blade_tables()]
    points = [blade_matrix(p) for p in (point_one, point_two)]
    forward_pairs = [pair_matrices(m.T) for m in points]
    backward_pairs = [pair_matrices(m) for m in points]
    biases = [jnp.concatenate([b, b]).reshape(1, PAIR) for b in (bias_one, bias_two)]

    def send_struct(g):
        return struct((4, 8, g.own, PAIR))

    def own_struct(g):
        return struct((8, g.own, PAIR))

    def rows_struct(g):
        return struct((g.pairs, PAIR))

    def part_scratch(g):
        return pltpu.VMEM((2, 4, 8 * g.own, C), BF)

    def scatter(values):
        return [lax.psum_scatter(v, "modes", scatter_dimension=0, tiled=False) for v in values]

    def gather_all(values):
        return [lax.all_gather(v, "modes", axis=0, tiled=False) for v in values]

    w2_scratch = pltpu.VMEM((KY, C, C), BF)

    def spectral(values, raw):
        return call(
            lambda *refs: spectral_kernel(*refs, groups=groups),
            [own_struct(g) for g in groups],
            [w2_scratch] + [part_scratch(g) for g in groups] * 2,
        )(*values, raw, spread, gather)

    def spectral_back(values, inputs, raw):
        out = call(
            lambda *refs: spectral_back_kernel(*refs, groups=groups),
            [own_struct(g) for g in groups] + [struct((8, C, PAIR), F32)],
            [w2_scratch] + [part_scratch(g) for g in groups] * 3,
        )(*values, *inputs, raw, spread, copies, unfold)
        return out[:2], out[2]

    send = [
        call(lambda *refs, g=g: first_kernel(*refs, group=g), send_struct(g), [field_scratch(g)])(
            a, t[0], m
        )
        for g, a, t, m in zip(groups, state, tables, matrices)
    ]
    spectrum_one = scatter(send)
    answer = gather_all(spectral(spectrum_one, spec_one))
    state_one, slope_one, send = zip(
        *[
            call(
                lambda *refs, g=g: middle_kernel(*refs, group=g),
                [rows_struct(g), rows_struct(g), send_struct(g)],
                [field_scratch(g)],
            )(y, a, *forward_pairs[0], biases[0], t[1], t[0], m, mt)
            for g, y, a, t, m, mt in zip(groups, answer, state, tables, matrices, matrices_t)
        ]
    )
    spectrum_two = scatter(send)
    answer = gather_all(spectral(spectrum_two, spec_two))
    sum_structs = [struct((2, 256, 256), F32), struct((8, PAIR), F32)]
    out, slopes_two, send, sums_two, bias_two_sum = zip(
        *[
            call(
                lambda *refs, g=g: turn_kernel(*refs, group=g),
                [rows_struct(g), rows_struct(g), send_struct(g)] + sum_structs,
                [field_scratch(g)],
            )(y, a, d, *forward_pairs[1], biases[1], t[1], t[2], m, mt)
            for g, y, a, d, t, m, mt in zip(
                groups, answer, state_one, grad, tables, matrices, matrices_t
            )
        ]
    )
    spectrum_grad, weight_two = spectral_back(scatter(send), spectrum_two, spec_two)
    answer = gather_all(spectrum_grad)
    grad_one, ds_one, send, sums_one, bias_one_sum = zip(
        *[
            call(
                lambda *refs, g=g: back_kernel(*refs, group=g),
                [rows_struct(g), rows_struct(g), send_struct(g)] + sum_structs,
                [field_scratch(g)],
            )(y, d2, d, sl, a, *backward_pairs[1], t[3], t[2], m, mt)
            for g, y, d2, d, sl, a, t, m, mt in zip(
                groups, answer, slopes_two, grad, slope_one, state, tables, matrices, matrices_t
            )
        ]
    )
    spectrum_grad, weight_one = spectral_back(scatter(send), spectrum_one, spec_one)
    answer = gather_all(spectrum_grad)
    result = [
        call(lambda *refs, g=g: last_kernel(*refs, group=g), rows_struct(g), [field_scratch(g)])(
            y, d, gr, *backward_pairs[0], t[3], mt
        )
        for g, y, d, gr, t, mt in zip(groups, answer, ds_one, grad_one, tables, matrices_t)
    ]
    ranks = lax.axis_size("dp")

    def reduce_spec(value):
        value = value.reshape(8, 4, CH, 2, 4, CH).transpose(0, 3, 4, 1, 2, 5)
        value = value.reshape(ranks, 64 // ranks, 4, CH, CH)
        value = lax.psum_scatter(value, "dp", scatter_dimension=0, tiled=False)
        return value.transpose(1, 0, 2, 3).reshape(4, -1)

    def reduce_point(sums, bias_sums):
        point = point_gradient(sums[0] + sums[1])
        bias = jnp.sum(bias_sums[0] + bias_sums[1], axis=0)
        return lax.psum((point, bias[:C] + bias[C:]), ("dp", "modes"))

    point_grad_two, bias_grad_two = reduce_point(sums_two, bias_two_sum)
    point_grad_one, bias_grad_one = reduce_point(sums_one, bias_one_sum)
    return (
        unpack(out[0], counts_big, groups[0], True),
        unpack(out[1], counts_small, groups[1], True),
        unpack(result[0], counts_big, groups[0], False),
        unpack(result[1], counts_small, groups[1], False),
        reduce_spec(weight_one),
        point_grad_one,
        bias_grad_one,
        reduce_spec(weight_two),
        point_grad_two,
        bias_grad_two,
    )


def solution(mesh):
    rows = P("dp", "modes", None)
    spec = P("modes", None, None, None, None)
    return jax.shard_map(
        local,
        mesh=mesh,
        in_specs=(rows, rows, P("dp"), P("dp"), P(), spec, P(), P(), spec, P(), P(), rows, rows),
        out_specs=(rows, rows, rows, rows, P("modes", "dp"), P(), P(), P("modes", "dp"), P(), P()),
        check_vma=False,
    )
```

```python
import math

import jax
import jax.numpy as jnp
import numpy as np
from jax import lax
from jax.experimental import pallas as pl
from jax.experimental.pallas import tpu as pltpu
from jax.sharding import PartitionSpec as P

BF, F32 = jnp.bfloat16, jnp.float32
KX = 16
KY = 16
C = 192
CH = 48
K = 32
PITCH = 40
PAIR = 2 * C
LIMIT = 62 * 2**20
SELECT = np.array([[0, 1, 2, 3], [1, 0, 3, 2], [2, 3, 0, 1], [3, 2, 1, 0]])
SIGNS = np.array(
    [[1.0, 1.0, 1.0, -1.0], [1.0, 1.0, 1.0, -1.0], [1.0, -1.0, 1.0, 1.0], [1.0, -1.0, 1.0, 1.0]]
)


def dot(a, b):
    return jnp.dot(a, b, preferred_element_type=F32)


def dot_nt(a, b):
    return lax.dot_general(a, b, (((1,), (1,)), ((), ())), preferred_element_type=F32)


def dot_tn(a, b):
    return lax.dot_general(a, b, (((0,), (0,)), ((), ())), preferred_element_type=F32)


def to_bf(values):
    return np.asarray(values, np.float32).astype(jnp.bfloat16)


def column_tables(height, width):
    position = np.arange(width)[:, None]
    frequency = np.arange(KY)[None, :]
    phase = ((position * frequency) % width).astype(np.float32) * np.float32(2.0 * math.pi / width)
    col = to_bf(np.stack([np.cos(phase), -np.sin(phase)], -1)).astype(np.float32)
    factor = np.where(np.arange(KY) == 0, 1.0, 2.0) / (height * width)
    inv = to_bf(col * factor[None, :, None].astype(np.float32)).astype(np.float32)
    half = width // 2

    def analysis_form(table):
        return to_bf(table.reshape(half, 2, KY, 2).transpose(3, 2, 1, 0).reshape(K, width))

    def synthesis_form(table):
        return to_bf(table.reshape(half, 2, KY, 2).transpose(0, 1, 3, 2).reshape(half, 2 * K))

    return analysis_form(col), synthesis_form(inv), analysis_form(inv), synthesis_form(col)


def blade_tables():
    eye = np.eye(CH)
    spread = np.zeros((4, C, C))
    gather = np.zeros((4, C, C))
    copies = np.zeros((4, C, C))
    unfold = np.zeros((4, C, C))
    for p in range(4):
        for b in range(4):
            q = int(np.where(SELECT[p] == b)[0][0])
            sign = SIGNS[p, q]
            at_p, at_q, at_b = (slice(i * CH, (i + 1) * CH) for i in (p, q, b))
            spread[p, at_q, at_b] = sign * eye
            unfold[p, at_b, at_q] = sign * eye
            gather[p, at_b, at_p] = eye
            copies[p, at_p, at_b] = eye
    return to_bf(spread), to_bf(gather), to_bf(copies), to_bf(unfold)


def mask_table(group):
    row = np.arange(8 * group.own)[:, None]
    lane = np.arange(C)[None, :]
    return (((row % group.own) // (group.own // 4)) == lane // CH).astype(np.float32)


def analysis(block, table):
    stacked = jnp.concatenate([block[:, :C], block[:, C:]], axis=0)
    return dot(table, stacked)


def put_field(field, n, value):
    field[0, pl.ds(pl.multiple_of(n * PITCH, 8), K), :] = value[:, :128]
    field[1, pl.ds(pl.multiple_of(n * PITCH, 8), K), 0:64] = value[:, 128:]


def get_rows(field, k, count):
    low = field[0, pl.ds(k, count, stride=PITCH), :]
    high = field[1, pl.ds(k, count, stride=PITCH), :]
    return jnp.concatenate([low, high[:, :64]], axis=1).astype(BF)


def rows_forward(field, matrix, ky2, count):
    parts = []
    for parity in range(2):
        ky = ky2 * 2 + parity
        parts.append(
            jnp.concatenate([get_rows(field, ky, count), get_rows(field, KY + ky, count)], axis=0)
        )
    return dot(matrix, jnp.concatenate(parts, axis=1))


def rows_inverse(field, matrix_t, spectrum, ky2, count):
    for parity in range(2):
        value = dot(matrix_t, spectrum[:, parity * C : (parity + 1) * C])
        ky = ky2 * 2 + parity
        for part in range(2):
            piece = value[part * count : (part + 1) * count]
            field[0, pl.ds(part * KY + ky, count, stride=PITCH), :] = piece[:, :128]
            field[1, pl.ds(part * KY + ky, count, stride=PITCH), :] = jnp.concatenate(
                [piece[:, 128:], jnp.zeros((count, 64), F32)], axis=1
            )


def synthesis(field, n, table):
    value = jnp.concatenate(
        [field[0, pl.ds(pl.multiple_of(n * PITCH, 8), K), :], field[1, pl.ds(pl.multiple_of(n * PITCH, 8), K), 0:64]], axis=1
    ).astype(BF)
    zero = jnp.zeros((K, C), BF)
    both = jnp.concatenate(
        [jnp.concatenate([value, zero], axis=1), jnp.concatenate([zero, value], axis=1)], axis=0
    )
    return dot(table, both)


def pointwise(block, first, second):
    left = dot(block[:, :256], first)
    right = dot(block[:, 128:], second)
    return jnp.concatenate(
        [left[:, :128], left[:, 128:] + right[:, :128], right[:, 128:]], axis=1
    )


def gelu_and_slope(value):
    cdf = 0.5 + 0.5 * lax.erf(value * (1.0 / math.sqrt(2.0)))
    bell = jnp.exp(-0.5 * value * value)
    return value * cdf, cdf + value * bell * (1.0 / math.sqrt(2.0 * math.pi))


class Group:
    def __init__(self, slots, rows, width, parts):
        self.slots, self.rows, self.width = slots, rows, width
        self.count = slots * rows
        self.half = width // 2
        self.pairs = self.count * self.half
        self.block = 1024 // self.half
        self.steps = self.count // self.block
        self.own = 4 * slots * 2
        self.full = parts * self.own


def struct(shape, dtype=BF):
    return jax.ShapeDtypeStruct(shape, dtype)


def loop(first, last, body, unroll=1):
    def step(i, carry):
        body(i)
        return carry

    lax.fori_loop(first, last, step, 0, unroll=unroll)


STEP = 16


def pack(source, target, group, live=None):
    for first in range(0, group.half, STEP):
        slabs = [
            source[:, j * PAIR : (j + 1) * PAIR] if live is None
            else source[:, j * PAIR : (j + 1) * PAIR] * live
            for j in range(first, first + STEP)
        ]
        target[:, first : first + STEP, :] = jnp.swapaxes(jnp.stack(slabs, axis=0), 0, 1)


def block_of(ref, group, i):
    rows = pl.ds(i * group.block, group.block)
    return ref[rows].reshape(group.block * group.half, PAIR)


def set_block(ref, group, i, value):
    rows = pl.ds(i * group.block, group.block)
    ref[rows] = value.reshape(group.block, group.half, PAIR)


def analyse(value, table, field, group, i):
    t = table[...]
    for q in range(group.block):
        put_field(
            field, i * group.block + q, analysis(value[q * group.half : (q + 1) * group.half], t)
        )


def synthesise(field, table, group, i):
    return jnp.concatenate(
        [synthesis(field, i * group.block + q, table[...]) for q in range(group.block)], axis=0
    )


def send_rows(field, matrix, out, group):
    def body(ky2):
        value = rows_forward(field, matrix[...], ky2, group.count).astype(BF)
        for owner in range(4):
            out[owner, ky2] = value[owner * group.own : (owner + 1) * group.own]

    loop(0, KY // 2, body, unroll=8)


def receive_rows(field, matrix_t, spectrum, group):
    def body(ky2):
        value = jnp.concatenate([spectrum[owner, ky2] for owner in range(4)], axis=0)
        rows_inverse(field, matrix_t[...], value, ky2, group.count)

    loop(0, KY // 2, body, unroll=8)


def build_weights(raw, w2):
    def body(ky):
        parts = [jnp.concatenate([raw[m, ky, b] for m in range(4)], axis=0) for b in range(4)]
        w2[ky] = jnp.concatenate(parts, axis=1)

    loop(0, KY, body, unroll=4)


def spread_rows(x, table, out, group, mask=None):
    rows = 8 * group.own
    value = x[...].reshape(rows, PAIR)
    for parity in range(2):
        part = value[:, parity * C : (parity + 1) * C]
        for p in range(4):
            result = dot(part, table[p])
            if mask is not None:
                result = result * mask[...]
            out[parity, p] = result.astype(BF)


def fold_rows(parts, table, out, index, group):
    halves = []
    for parity in range(2):
        total = None
        for p in range(4):
            term = dot(parts[parity, p], table[p])
            total = term if total is None else total + term
        halves.append(total)
    out[index] = jnp.concatenate(halves, axis=1).astype(BF).reshape(8, group.own, PAIR)


def ky_rows(parts, parity, ky2, group):
    rows = pl.ds(pl.multiple_of(ky2 * group.own, group.own), group.own)
    return jnp.concatenate([parts[parity, p, rows, :] for p in range(4)], axis=0)


def set_ky_rows(parts, parity, ky2, group, value):
    rows = pl.ds(pl.multiple_of(ky2 * group.own, group.own), group.own)
    for p in range(4):
        parts[parity, p, rows, :] = value[p * group.own : (p + 1) * group.own]


def spectral_forward(x, w2, spread, gather, mask, l, z, out, index, group):
    spread_rows(x, spread, l, group)

    def body(ky2):
        for parity in range(2):
            value = dot_nt(ky_rows(l, parity, ky2, group), w2[ky2 * 2 + parity])
            value = (value * mask[0 : 4 * group.own, :]).astype(BF)
            set_ky_rows(z, parity, ky2, group, value)

    loop(0, KY // 2, body, unroll=4)
    fold_rows(z, gather, out, index, group)


def spectral_backward(d, x, w2, spread, copies, unfold, mask, l, a, z, out, index, group):
    spread_rows(x, spread, l, group)
    spread_rows(d, copies, a, group, mask)

    def body(ky2):
        for parity in range(2):
            value = dot(ky_rows(a, parity, ky2, group), w2[ky2 * 2 + parity])
            set_ky_rows(z, parity, ky2, group, value.astype(BF))

    loop(0, KY // 2, body, unroll=4)
    fold_rows(z, unfold, out, index, group)


def weight_gradients(a, l, out, groups):
    def body(ky2):
        grads = []
        for parity in range(2):
            left = jnp.concatenate([ky_rows(a[g], parity, ky2, groups[g]) for g in range(2)], axis=0)
            right = jnp.concatenate([ky_rows(l[g], parity, ky2, groups[g]) for g in range(2)], axis=0)
            grads.append(dot_tn(left, right))
        out[ky2] = jnp.concatenate(grads, axis=1).astype(BF)

    loop(0, KY // 2, body, unroll=2)


def point_sums(ds, a, sums, bias_sum):
    sums[0] += dot_tn(ds[:, :256], a[:, :256])
    sums[1] += dot_tn(ds[:, 128:], a[:, 128:])
    bias_sum[...] += jnp.sum(ds.astype(F32).reshape(-1, 8, PAIR), axis=0)


def fold_point(sums, bias_sum, out):
    total = sums[0][:C, :C] + sums[1][64:, 64:]
    grad = None
    for p in range(4):
        row = total[p * CH : (p + 1) * CH]
        pieces = []
        for b in range(4):
            q = int(np.where(SELECT[p] == b)[0][0])
            piece = row[:, q * CH : (q + 1) * CH]
            pieces.append(piece if SIGNS[p, q] > 0 else -piece)
        term = jnp.concatenate(pieces, axis=1)
        grad = term if grad is None else grad + term
    bias = bias_sum[...]
    bias = jnp.sum(bias[:, :C] + bias[:, C:], axis=0, keepdims=True)
    first = lax.broadcasted_iota(jnp.int32, (16, C), 0) == 0
    for k in range(3):
        out[k, :, 0:C] = grad[k * 16 : (k + 1) * 16]
    out[3, :, 0:C] = jnp.where(first, jnp.broadcast_to(bias, (16, C)), 0.0)


class Refs:
    pass


def main_kernel(names, groups, ranks, *refs):
    r = Refs()
    for name, ref in zip(names, refs, strict=True):
        setattr(r, name, ref)
    reduce_here = ranks == 8
    me = lax.axis_index("modes")
    rank = lax.axis_index("dp")

    def mode_device(d):
        return (rank, lax.rem(me + d, 4))

    def rank_device(d):
        return (lax.rem(rank + d, ranks), me)

    def local_copy(source, target, sem):
        copy = pltpu.make_async_copy(source, target, sem)
        copy.start()
        return copy

    def remote(source, target, send, recv, device):
        copy = pltpu.make_async_remote_copy(
            src_ref=source,
            dst_ref=target,
            send_sem=send,
            recv_sem=recv,
            device_id=device,
            device_id_type=pl.DeviceIdType.MESH,
        )
        copy.start()
        return copy

    ins = [r.grids0, r.grids1]
    cots = [r.cot0, r.cot1]
    stage = [r.stage0, r.stage1]
    a0, a1 = [r.a00, r.a01], [r.a10, r.a11]
    slope, grad, delta = [r.sl0, r.sl1], [r.g0, r.g1], [r.d0, r.d1]
    field = [r.field0, r.field1]
    send, recv, full = [r.send0, r.send1], [r.recv0, r.recv1], [r.full0, r.full1]
    x1, x2, dy = [r.x10, r.x11], [r.x20, r.x21], [r.dy0, r.dy1]
    l, a, z = [r.l0, r.l1], [r.a_0, r.a_1], [r.z0, r.z1]
    mask = [r.mask0, r.mask1]
    matrix, matrix_t = [r.m0, r.m1], [r.mt0, r.mt1]
    tables = [[getattr(r, f"t{g}{k}") for k in range(4)] for g in range(2)]
    forward = [(r.fa1, r.fb1), (r.fa2, r.fb2)]
    backward = [(r.ba1, r.bb1), (r.ba2, r.bb2)]
    bias = [r.bias1, r.bias2]
    counts = [r.count0, r.count1]
    order = (1, 0)

    loads = {}
    for g in order:
        loads[g] = local_copy(ins[g], stage[g], r.in_sem.at[g])
    raw_load = local_copy(r.spec1, r.raw, r.in_sem.at[2])

    barrier = pltpu.get_barrier_semaphore()
    for d in range(1, 4):
        pl.semaphore_signal(barrier, inc=1, device_id=mode_device(d), device_id_type=pl.DeviceIdType.MESH)
    if reduce_here:
        for d in range(1, ranks):
            pl.semaphore_signal(barrier, inc=1, device_id=rank_device(d), device_id_type=pl.DeviceIdType.MESH)
    pl.semaphore_wait(barrier, 3 + (ranks - 1 if reduce_here else 0))

    scatters, gathers = {}, {}

    def start_scatter(g):
        send_rows(field[g], matrix[g], send[g], groups[g])
        scatters[g] = [
            remote(
                send[g].at[lax.rem(me + d, 4)],
                recv[g].at[d - 1],
                r.rs_send.at[g, d - 1],
                r.rs_recv.at[g, d - 1],
                mode_device(d),
            )
            for d in range(1, 4)
        ]

    def end_scatter(g, out):
        for copy in scatters[g]:
            copy.wait()
        total = send[g][me].astype(F32)
        for d in range(3):
            total = total + recv[g][d].astype(F32)
        out[...] = total.astype(BF)

    def start_gather(g):
        gathers[g] = [
            remote(
                full[g].at[me],
                full[g].at[me],
                r.ag_send.at[g, d - 1],
                r.ag_recv.at[g, d - 1],
                mode_device(d),
            )
            for d in range(1, 4)
        ]

    def end_gather(g):
        for copy in gathers[g]:
            copy.wait()
        receive_rows(field[g], matrix_t[g], full[g], groups[g])

    def spectral(g, layer):
        x = (x1, x2)[layer][g]
        end_scatter(g, x)
        w2 = (r.w21, r.w22)[layer]
        spectral_forward(x, w2, r.spread, r.gather, mask[g], l[g], z[g], full[g], me, groups[g])
        start_gather(g)

    def spectral_back(g, layer):
        x = (x1, x2)[layer][g]
        end_scatter(g, dy[g])
        w2 = (r.w21, r.w22)[layer]
        spectral_backward(
            dy[g], x, w2, r.spread, r.copies, r.unfold, mask[g], l[g], a[g], z[g], full[g], me, groups[g]
        )
        start_gather(g)

    dw_copies = {}

    def start_weights(layer):
        out = (r.dw1, r.dw2)[layer]
        weight_gradients(a, l, out, groups)
        if reduce_here:
            dw_copies[layer] = [
                remote(
                    out.at[lax.rem(rank + d, ranks)],
                    (r.dwr1, r.dwr2)[layer].at[d - 1],
                    r.dw_send.at[layer, d - 1],
                    r.dw_recv.at[layer, d - 1],
                    rank_device(d),
                )
                for d in range(1, ranks)
            ]

    writes = []

    def end_weights(layer):
        out = (r.dw1, r.dw2)[layer]
        if not reduce_here:
            writes.append(local_copy(out, (r.spec_out1, r.spec_out2)[layer], r.out_sem.at[4 + layer]))
            return
        for copy in dw_copies[layer]:
            copy.wait()
        total = out[rank].astype(F32)
        for d in range(ranks - 1):
            total = total + (r.dwr1, r.dwr2)[layer][d].astype(F32)
        r.dws[layer] = total
        writes.append(local_copy(r.dws.at[layer], (r.spec_out1, r.spec_out2)[layer], r.out_sem.at[4 + layer]))

    point_copies = {}

    def point_first(layer):
        fold_point(r.sums.at[layer], r.bias_sum.at[layer], r.pt_send.at[layer])
        if reduce_here:
            point_copies[layer] = [
                remote(
                    r.pt_send.at[layer, lax.rem(me + d, 4)],
                    r.pt_one.at[layer, d - 1],
                    r.pt_sems.at[layer, 0, d - 1],
                    r.pt_sems.at[layer, 1, d - 1],
                    mode_device(d),
                )
                for d in range(1, 4)
            ]

    def point_second(layer):
        if not reduce_here:
            return
        for copy in point_copies[layer]:
            copy.wait()
        total = r.pt_send[layer, me]
        for d in range(3):
            total = total + r.pt_one[layer, d]
        r.pt_two[layer, rank] = total
        point_copies[layer] = [
            remote(
                r.pt_two.at[layer, rank],
                r.pt_two.at[layer, rank],
                r.pt_sems.at[layer, 2, d - 1],
                r.pt_sems.at[layer, 3, d - 1],
                rank_device(d),
            )
            for d in range(1, ranks)
        ]

    def point_third(layer):
        if not reduce_here:
            return
        for copy in point_copies[layer]:
            copy.wait()
        total = r.pt_two[layer, 0]
        for k in range(1, ranks):
            total = total + r.pt_two[layer, k]
        r.pt_full[layer, me] = total
        point_copies[layer] = [
            remote(
                r.pt_full.at[layer, me],
                r.pt_full.at[layer, me],
                r.pt_sems.at[layer, 4, d - 1],
                r.pt_sems.at[layer, 5, d - 1],
                mode_device(d),
            )
            for d in range(1, 4)
        ]

    def point_last(layer):
        source = r.pt_full if reduce_here else r.pt_send
        if reduce_here:
            for copy in point_copies[layer]:
                copy.wait()
        writes.append(local_copy(source.at[layer], (r.point_out1, r.point_out2)[layer], r.out_sem.at[6 + layer]))

    for g in order:
        group = groups[g]
        loads[g].wait()
        pack(stage[g], a0[g], group)
        loads[g] = local_copy(cots[g], stage[g], r.in_sem.at[g])
        loop(0, group.steps, lambda i, g=g: analyse(block_of(a0[g], groups[g], i), tables[g][0], field[g], groups[g], i))
        start_scatter(g)
    raw_load.wait()
    build_weights(r.raw, r.w21)
    raw_load = local_copy(r.spec2, r.raw, r.in_sem.at[2])

    def pack_grad(g):
        group = groups[g]
        loads[g].wait()
        slot = lax.broadcasted_iota(jnp.int32, (group.count, PAIR), 0) // group.rows
        live = (slot < counts[g][0]).astype(F32).astype(BF)
        pack(stage[g], grad[g], group, live)

    spectral(1, 0)
    pack_grad(1)
    spectral(0, 0)
    pack_grad(0)
    raw_load.wait()
    build_weights(r.raw, r.w22)
    r.sums[...] = jnp.zeros_like(r.sums)
    r.bias_sum[...] = jnp.zeros_like(r.bias_sum)
    r.pt_send[...] = jnp.zeros_like(r.pt_send)

    def middle(g, first, last):
        group = groups[g]

        def body(i):
            x = block_of(a0[g], group, i)
            s = synthesise(field[g], tables[g][1], group, i) + pointwise(x, forward[0][0][...], forward[0][1][...]) + bias[0][...]
            gelu, sl = gelu_and_slope(s)
            value = (x.astype(F32) + gelu).astype(BF)
            set_block(a1[g], group, i, value)
            set_block(slope[g], group, i, sl.astype(BF))
            analyse(value, tables[g][0], field[g], group, i)

        loop(first, last, body)

    def turn(g, first, last):
        group = groups[g]

        def body(i):
            x = block_of(a1[g], group, i)
            s = synthesise(field[g], tables[g][1], group, i) + pointwise(x, forward[1][0][...], forward[1][1][...]) + bias[1][...]
            gelu, sl = gelu_and_slope(s)
            d = (block_of(grad[g], group, i).astype(F32) * sl).astype(BF)
            set_block(a1[g], group, i, (x.astype(F32) + gelu).astype(BF))
            set_block(delta[g], group, i, d)
            point_sums(d, x, r.sums.at[1], r.bias_sum.at[1])
            analyse(d, tables[g][2], field[g], group, i)

        loop(first, last, body)

    def back(g, first, last):
        group = groups[g]

        def body(i):
            g1 = (
                synthesise(field[g], tables[g][3], group, i)
                + pointwise(block_of(delta[g], group, i), backward[1][0][...], backward[1][1][...])
                + block_of(grad[g], group, i).astype(F32)
            )
            set_block(grad[g], group, i, g1.astype(BF))
            d = (g1 * block_of(slope[g], group, i).astype(F32)).astype(BF)
            set_block(delta[g], group, i, d)
            point_sums(d, block_of(a0[g], group, i), r.sums.at[0], r.bias_sum.at[0])
            analyse(d, tables[g][2], field[g], group, i)

        loop(first, last, body)

    def final(g, first, last):
        group = groups[g]

        def body(i):
            value = (
                synthesise(field[g], tables[g][3], group, i)
                + pointwise(block_of(delta[g], group, i), backward[0][0][...], backward[0][1][...])
                + block_of(grad[g], group, i).astype(F32)
            )
            set_block(grad[g], group, i, value.astype(BF))

        loop(first, last, body)

    big, small = groups[0].steps, groups[1].steps
    end_gather(1)
    middle(1, 0, small)
    start_scatter(1)
    end_gather(0)
    middle(0, 0, big // 2)
    spectral(1, 1)
    middle(0, big // 2, big)
    start_scatter(0)

    end_gather(1)
    turn(1, 0, small // 2)
    spectral(0, 1)
    turn(1, small // 2, small)
    start_scatter(1)
    writes.append(local_copy(a1[1], r.out1, r.out_sem.at[1]))
    end_gather(0)
    turn(0, 0, big // 2)
    spectral_back(1, 1)
    turn(0, big // 2, big)
    start_scatter(0)
    writes.append(local_copy(a1[0], r.out0, r.out_sem.at[0]))
    point_first(1)

    end_gather(1)
    back(1, 0, small // 2)
    spectral_back(0, 1)
    start_weights(1)
    back(1, small // 2, small)
    start_scatter(1)
    point_second(1)
    end_gather(0)
    back(0, 0, big // 2)
    spectral_back(1, 0)
    back(0, big // 2, big)
    start_scatter(0)
    point_first(0)
    point_third(1)

    end_gather(1)
    final(1, 0, small // 2)
    spectral_back(0, 0)
    start_weights(0)
    point_second(0)
    final(1, small // 2, small)
    writes.append(local_copy(grad[1], r.back1, r.out_sem.at[3]))
    point_last(1)
    end_weights(1)
    end_gather(0)
    final(0, 0, big)
    writes.append(local_copy(grad[0], r.back0, r.out_sem.at[2]))
    point_third(0)
    end_weights(0)
    point_last(0)
    for copy in writes:
        copy.wait()


def finish_kernel(count, out_in, back_in, out, back, *, group):
    rows = group.count
    slot = lax.broadcasted_iota(jnp.int32, (rows, PAIR), 0) // group.rows
    live = (slot < count[0]).astype(F32).astype(BF)
    for source, target in ((out_in, out), (back_in, back)):
        value = jnp.swapaxes(source[...], 0, 1)
        for j in range(STEP):
            slab = value[j]
            target[:, j * PAIR : (j + 1) * PAIR] = slab * live if target is out else slab


def finish(count, out, back, group):
    width = group.width * C
    source = pl.BlockSpec((group.count, STEP, PAIR), lambda i: (0, i, 0))
    target = pl.BlockSpec((group.count, STEP * PAIR), lambda i: (0, i))
    result = pl.pallas_call(
        lambda *refs: finish_kernel(*refs, group=group),
        grid=(group.half // STEP,),
        in_specs=[pl.BlockSpec(memory_space=pltpu.SMEM), source, source],
        out_specs=[target, target],
        out_shape=[struct((group.count, width))] * 2,
        compiler_params=pltpu.CompilerParams(vmem_limit_bytes=LIMIT),
    )(count, out, back)
    return [v.reshape(group.slots, group.rows, width) for v in result]


def blade_matrix(weight):
    rows = [
        jnp.concatenate(
            [weight[int(SELECT[p, q])] * float(SIGNS[p, q]) for q in range(4)], axis=1
        )
        for p in range(4)
    ]
    return jnp.concatenate(rows, axis=0)


def pair_matrices(matrix):
    both = jnp.pad(matrix, ((0, C), (0, C))) + jnp.pad(matrix, ((C, 0), (C, 0)))
    corner = np.ones((256, 256), np.float32)
    corner[:128, :128] = 0.0
    return both[:256, :256], both[128:, 128:] * corner.astype(both.dtype)


def row_matrix(mode_table, group, place, parts):
    height = group.rows * parts
    frequency = np.arange(KX)
    frequency = np.where(frequency < KX // 2, frequency, frequency - KX)
    phase = (frequency[:, None] * np.arange(height)[None, :]) % height
    phase = phase.astype(np.float32) * np.float32(2.0 * math.pi / height)
    table = jnp.asarray(np.stack([np.cos(phase), np.sin(phase)], 1).astype(np.float32))
    table = lax.dynamic_slice_in_dim(table, place * group.rows, group.rows, axis=2)[mode_table]
    cosine, sine = table[:, 0], table[:, 1]
    both = jnp.stack([jnp.stack([cosine, sine], 1), jnp.stack([-sine, cosine], 1)], 1)
    eye = jnp.eye(group.slots, dtype=F32)
    full = both[:, None, :, :, None, :] * eye[None, :, None, None, :, None]
    return full.reshape(KX * group.slots * 2, 2 * group.count).astype(BF)


def local(
    grids_big,
    grids_small,
    counts_big,
    counts_small,
    mode_table,
    spec_one,
    point_one,
    bias_one,
    spec_two,
    point_two,
    bias_two,
    cot_big,
    cot_small,
):
    parts = lax.axis_size("modes")
    ranks = lax.axis_size("dp")
    place = lax.axis_index("modes")
    reduce_here = ranks == 8
    groups = [
        Group(g.shape[0], g.shape[1], g.shape[2] // C, parts) for g in (grids_big, grids_small)
    ]
    inputs, outputs, scratch = {}, {}, {}
    smem, vmem, hbm = pltpu.SMEM, pltpu.VMEM, pl.ANY
    inputs["count0"] = (counts_big, smem)
    inputs["count1"] = (counts_small, smem)
    arrays = ((grids_big, cot_big), (grids_small, cot_small))
    spread, gather, copies, unfold = blade_tables()
    for g, group in enumerate(groups):
        flat = (group.count, group.width * C)
        inputs[f"grids{g}"] = (arrays[g][0].reshape(flat), hbm)
        inputs[f"cot{g}"] = (arrays[g][1].reshape(flat), hbm)
        for k, table in enumerate(column_tables(group.rows * parts, group.width)):
            inputs[f"t{g}{k}"] = (jnp.asarray(table), vmem)
        matrix = row_matrix(mode_table, group, place, parts)
        inputs[f"m{g}"] = (matrix, vmem)
        inputs[f"mt{g}"] = (matrix.T, vmem)
        inputs[f"mask{g}"] = (jnp.asarray(mask_table(group)), vmem)
        rows = (group.count, group.half, PAIR)
        outputs[f"out{g}"] = struct(rows)
        outputs[f"back{g}"] = struct(rows)
        scratch[f"stage{g}"] = pltpu.VMEM(flat, BF)
        for name in ("a0", "a1", "sl", "g", "d"):
            scratch[f"{name}{g}"] = pltpu.VMEM(rows, BF)
        scratch[f"field{g}"] = pltpu.VMEM((2, group.count * PITCH, 128), F32)
        for name, lead in (("send", 4), ("recv", 3), ("full", 4)):
            scratch[f"{name}{g}"] = pltpu.VMEM((lead, 8, group.own, PAIR), BF)
        for name in ("x1", "x2", "dy"):
            scratch[f"{name}{g}"] = pltpu.VMEM((8, group.own, PAIR), BF)
        for name in ("l", "a_", "z"):
            scratch[f"{name}{g}"] = pltpu.VMEM((2, 4, 8 * group.own, C), BF)
    for name, table in (("spread", spread), ("gather", gather), ("copies", copies), ("unfold", unfold)):
        inputs[name] = (jnp.asarray(table), vmem)
    layers = ((point_one, bias_one, spec_one), (point_two, bias_two, spec_two))
    for k, (point, bias, spec) in enumerate(layers, 1):
        matrix = blade_matrix(point)
        inputs[f"fa{k}"], inputs[f"fb{k}"] = [(v, vmem) for v in pair_matrices(matrix.T)]
        inputs[f"ba{k}"], inputs[f"bb{k}"] = [(v, vmem) for v in pair_matrices(matrix)]
        inputs[f"bias{k}"] = (jnp.concatenate([bias, bias]).reshape(1, PAIR), vmem)
        inputs[f"spec{k}"] = (spec, hbm)
        outputs[f"spec_out{k}"] = struct((C, PAIR), F32) if reduce_here else struct((8, C, PAIR))
        outputs[f"point_out{k}"] = struct((4, 16, 256), F32)
        scratch[f"w2{k}"] = pltpu.VMEM((KY, C, C), BF)
        scratch[f"dw{k}"] = pltpu.VMEM((8, C, PAIR), BF)
        if reduce_here:
            scratch[f"dwr{k}"] = pltpu.VMEM((ranks - 1, C, PAIR), BF)
    scratch["raw"] = pltpu.VMEM(spec_one.shape, BF)
    scratch["sums"] = pltpu.VMEM((2, 2, 256, 256), F32)
    scratch["bias_sum"] = pltpu.VMEM((2, 8, PAIR), F32)
    scratch["pt_send"] = pltpu.VMEM((2, 4, 16, 256), F32)
    dma = pltpu.SemaphoreType.DMA
    if reduce_here:
        scratch["dws"] = pltpu.VMEM((2, C, PAIR), F32)
        scratch["pt_one"] = pltpu.VMEM((2, 3, 16, 256), F32)
        scratch["pt_two"] = pltpu.VMEM((2, ranks, 16, 256), F32)
        scratch["pt_full"] = pltpu.VMEM((2, 4, 16, 256), F32)
        scratch["dw_send"] = dma((2, ranks - 1))
        scratch["dw_recv"] = dma((2, ranks - 1))
        scratch["pt_sems"] = dma((2, 6, ranks - 1))
    for name in ("rs_send", "rs_recv", "ag_send", "ag_recv"):
        scratch[name] = dma((2, 3))
    scratch["in_sem"] = dma((3,))
    scratch["out_sem"] = dma((8,))
    names = list(inputs) + list(outputs) + list(scratch)
    result = pl.pallas_call(
        lambda *refs: main_kernel(names, groups, ranks, *refs),
        in_specs=[pl.BlockSpec(memory_space=space) for _, space in inputs.values()],
        out_specs=[pl.BlockSpec(memory_space=hbm)] * len(outputs),
        out_shape=list(outputs.values()),
        scratch_shapes=list(scratch.values()),
        compiler_params=pltpu.CompilerParams(
            vmem_limit_bytes=LIMIT, collective_id=0, has_side_effects=True
        ),
    )(*[value for value, _ in inputs.values()])
    result = dict(zip(outputs, result))
    out_big, back_big = finish(counts_big, result["out0"], result["back0"], groups[0])
    out_small, back_small = finish(counts_small, result["out1"], result["back1"], groups[1])

    def spec_gradient(value):
        if reduce_here:
            return value.reshape(4, CH, 2, 4, CH).transpose(0, 2, 3, 1, 4).reshape(4, -1)
        value = value.reshape(8, 4, CH, 2, 4, CH).transpose(0, 3, 4, 1, 2, 5)
        value = value.reshape(ranks, 64 // ranks, 4, CH, CH).astype(F32)
        value = lax.psum_scatter(value, "dp", scatter_dimension=0, tiled=False)
        return value.transpose(1, 0, 2, 3).reshape(4, -1)

    grads = []
    for k in (1, 2):
        point = result[f"point_out{k}"]
        if not reduce_here:
            point = lax.psum(point, ("dp", "modes"))
        point = point.reshape(64, 256)
        weight = point[:CH, :C].reshape(CH, 4, CH).transpose(1, 0, 2)
        grads += [spec_gradient(result[f"spec_out{k}"]), weight, point[CH, :C]]
    return (out_big, out_small, back_big, back_small, *grads)


def solution(mesh):
    rows = P("dp", "modes", None)
    spec = P("modes", None, None, None, None)
    return jax.shard_map(
        local,
        mesh=mesh,
        in_specs=(rows, rows, P("dp"), P("dp"), P(), spec, P(), P(), spec, P(), P(), rows, rows),
        out_specs=(rows, rows, rows, rows, P("modes", "dp"), P(), P(), P("modes", "dp"), P(), P()),
        check_vma=False,
    )
```

```python
import math

import jax
import jax.numpy as jnp
import numpy as np
from jax import lax
from jax.experimental import pallas as pl
from jax.experimental.pallas import tpu as pltpu
from jax.sharding import PartitionSpec as P

BF, F32 = jnp.bfloat16, jnp.float32
KX = 16
KY = 16
C = 192
CH = 48
K = 32
PITCH = 40
PAIR = 2 * C
LIMIT = 62 * 2**20
SELECT = np.array([[0, 1, 2, 3], [1, 0, 3, 2], [2, 3, 0, 1], [3, 2, 1, 0]])
SIGNS = np.array(
    [[1.0, 1.0, 1.0, -1.0], [1.0, 1.0, 1.0, -1.0], [1.0, -1.0, 1.0, 1.0], [1.0, -1.0, 1.0, 1.0]]
)


def dot(a, b):
    return jnp.dot(a, b, preferred_element_type=F32)


def dot_nt(a, b):
    return lax.dot_general(a, b, (((1,), (1,)), ((), ())), preferred_element_type=F32)


def dot_tn(a, b):
    return lax.dot_general(a, b, (((0,), (0,)), ((), ())), preferred_element_type=F32)


def to_bf(values):
    return np.asarray(values, np.float32).astype(jnp.bfloat16)


def column_tables(height, width):
    position = np.arange(width)[:, None]
    frequency = np.arange(KY)[None, :]
    phase = ((position * frequency) % width).astype(np.float32) * np.float32(2.0 * math.pi / width)
    col = to_bf(np.stack([np.cos(phase), -np.sin(phase)], -1)).astype(np.float32)
    factor = np.where(np.arange(KY) == 0, 1.0, 2.0) / (height * width)
    inv = to_bf(col * factor[None, :, None].astype(np.float32)).astype(np.float32)
    half = width // 2

    def analysis_form(table):
        return to_bf(table.reshape(half, 2, KY, 2).transpose(3, 2, 1, 0).reshape(K, width))

    def synthesis_form(table):
        return to_bf(table.reshape(half, 2, KY, 2).transpose(0, 1, 3, 2).reshape(half, 2 * K))

    return analysis_form(col), synthesis_form(inv), analysis_form(inv), synthesis_form(col)


def blade_tables():
    eye = np.eye(CH)
    spread = np.zeros((4, C, C))
    gather = np.zeros((4, C, C))
    copies = np.zeros((4, C, C))
    unfold = np.zeros((4, C, C))
    for p in range(4):
        for b in range(4):
            q = int(np.where(SELECT[p] == b)[0][0])
            sign = SIGNS[p, q]
            at_p, at_q, at_b = (slice(i * CH, (i + 1) * CH) for i in (p, q, b))
            spread[p, at_q, at_b] = sign * eye
            unfold[p, at_b, at_q] = sign * eye
            gather[p, at_b, at_p] = eye
            copies[p, at_p, at_b] = eye
    return to_bf(spread), to_bf(gather), to_bf(copies), to_bf(unfold)


def mask_table(group):
    row = np.arange(8 * group.own)[:, None]
    lane = np.arange(C)[None, :]
    return (((row % group.own) // (group.own // 4)) == lane // CH).astype(np.float32)


def analysis(block, table):
    stacked = jnp.concatenate([block[:, :C], block[:, C:]], axis=0)
    return dot(table, stacked)


def put_field(field, n, value):
    field[0, pl.ds(pl.multiple_of(n * PITCH, 8), K), :] = value[:, :128]
    field[1, pl.ds(pl.multiple_of(n * PITCH, 8), K), 0:64] = value[:, 128:]


def get_rows(field, k, count):
    low = field[0, pl.ds(k, count, stride=PITCH), :]
    high = field[1, pl.ds(k, count, stride=PITCH), :]
    return jnp.concatenate([low, high[:, :64]], axis=1).astype(BF)


def rows_forward(field, matrix, ky2, count):
    parts = []
    for parity in range(2):
        ky = ky2 * 2 + parity
        parts.append(
            jnp.concatenate([get_rows(field, ky, count), get_rows(field, KY + ky, count)], axis=0)
        )
    return dot(matrix, jnp.concatenate(parts, axis=1))


def rows_inverse(field, matrix_t, spectrum, ky2, count):
    for parity in range(2):
        value = dot(matrix_t, spectrum[:, parity * C : (parity + 1) * C])
        ky = ky2 * 2 + parity
        for part in range(2):
            piece = value[part * count : (part + 1) * count]
            field[0, pl.ds(part * KY + ky, count, stride=PITCH), :] = piece[:, :128]
            field[1, pl.ds(part * KY + ky, count, stride=PITCH), :] = jnp.concatenate(
                [piece[:, 128:], jnp.zeros((count, 64), F32)], axis=1
            )


def synthesis(field, n, table):
    value = jnp.concatenate(
        [field[0, pl.ds(pl.multiple_of(n * PITCH, 8), K), :], field[1, pl.ds(pl.multiple_of(n * PITCH, 8), K), 0:64]], axis=1
    ).astype(BF)
    zero = jnp.zeros((K, C), BF)
    both = jnp.concatenate(
        [jnp.concatenate([value, zero], axis=1), jnp.concatenate([zero, value], axis=1)], axis=0
    )
    return dot(table, both)


def pointwise(block, first, second, product):
    left = product(block[:, :256], first)
    right = product(block[:, 128:], second)
    return jnp.concatenate(
        [left[:, :128], left[:, 128:] + right[:, :128], right[:, 128:]], axis=1
    )


def gelu_and_slope(value):
    cdf = 0.5 + 0.5 * lax.erf(value * (1.0 / math.sqrt(2.0)))
    bell = jnp.exp(-0.5 * value * value)
    return value * cdf, cdf + value * bell * (1.0 / math.sqrt(2.0 * math.pi))


class Group:
    def __init__(self, kind, first, slots, rows, width, parts):
        self.kind, self.first = kind, first
        self.slots, self.rows, self.width = slots, rows, width
        self.count = slots * rows
        self.half = width // 2
        self.block = 1024 // self.half
        self.steps = self.count // self.block
        self.own = 4 * slots * 2
        self.lines = 8 * self.own
        self.stack = max(1, 16 // self.own)
        self.dtype = F32 if self.own % 16 else BF


def struct(shape, dtype=BF):
    return jax.ShapeDtypeStruct(shape, dtype)


def loop(first, last, body, unroll=1):
    def step(i, carry):
        body(i)
        return carry

    lax.fori_loop(first, last, step, 0, unroll=unroll)


STEP = 16


def pack(source, target, group, live=None):
    rows = slice(group.first, group.first + group.count)
    for first in range(0, group.half, STEP):
        slabs = []
        for j in range(first, first + STEP):
            slab = source[rows, j * PAIR : (j + 1) * PAIR]
            slabs.append(slab if live is None else slab * live)
        target[rows, first : first + STEP, :] = jnp.swapaxes(jnp.stack(slabs, axis=0), 0, 1)


def block_of(ref, group, i):
    rows = pl.ds(group.first + i * group.block, group.block)
    return ref[rows].reshape(group.block * group.half, PAIR)


def set_block(ref, group, i, value):
    rows = pl.ds(group.first + i * group.block, group.block)
    ref[rows] = value.reshape(group.block, group.half, PAIR)


def analyse(value, table, field, group, i):
    t = table[...]
    for q in range(group.block):
        put_field(
            field, i * group.block + q, analysis(value[q * group.half : (q + 1) * group.half], t)
        )


def synthesise(field, table, group, i):
    return jnp.concatenate(
        [synthesis(field, i * group.block + q, table[...]) for q in range(group.block)], axis=0
    )


def send_rows(field, matrix, out, group):
    def body(k):
        values = [
            rows_forward(field, matrix[...], k * group.stack + j, group.count)
            for j in range(group.stack)
        ]
        rows = pl.ds(pl.multiple_of(k * 16, 16), 16)
        for owner in range(4):
            block = slice(owner * group.own, (owner + 1) * group.own)
            piece = jnp.concatenate([v[block] for v in values], axis=0)
            out[owner % 2, owner // 2, rows, :] = piece.astype(BF)

    count = 8 // group.stack
    loop(0, count, body, unroll=count)


def receive_rows(field, matrix_t, spectrum, group):
    def body(k):
        rows = pl.ds(pl.multiple_of(k * 16, 16), 16)
        pieces = [spectrum[owner, rows, :] for owner in range(4)]
        if group.stack > 1:
            pieces = [p.astype(F32) for p in pieces]
        for j in range(group.stack):
            block = slice(j * group.own, (j + 1) * group.own)
            value = jnp.concatenate([p[block] for p in pieces], axis=0).astype(BF)
            rows_inverse(field, matrix_t[...], value, k * group.stack + j, group.count)

    count = 8 // group.stack
    loop(0, count, body, unroll=count)


def build_weights(raw, w2):
    def body(ky):
        parts = [jnp.concatenate([raw[m, ky, b] for m in range(4)], axis=0) for b in range(4)]
        w2[ky] = jnp.concatenate(parts, axis=1)

    loop(0, KY, body, unroll=4)


def build_point(point, first, second):
    rows = []
    for p in range(4):
        pieces = []
        for q in range(4):
            piece = point[int(SELECT[p, q])]
            pieces.append(piece if SIGNS[p, q] > 0 else -piece)
        rows.append(jnp.concatenate(pieces, axis=1))
    matrix = jnp.concatenate(rows, axis=0)
    zero = jnp.zeros((C, C), BF)
    both = jnp.concatenate(
        [jnp.concatenate([matrix, zero], axis=1), jnp.concatenate([zero, matrix], axis=1)], axis=0
    )
    first[...] = both[:256, :256]
    second[...] = both[128:, 128:]
    second[0:128, 0:128] = jnp.zeros((128, 128), BF)


def build_rows(modes, table, table_t, place, matrix, matrix_t, group):
    size = KX * group.slots * 2
    per = group.slots * 2
    row = lax.broadcasted_iota(jnp.int32, (size, size), 0)
    lane = lax.broadcasted_iota(jnp.int32, (size, size), 1)
    wanted = jnp.zeros((size, size), jnp.int32)
    for m in range(KX):
        inside = jnp.logical_and(row >= m * per, row < (m + 1) * per)
        wanted = jnp.where(inside, modes[m] * per + row - m * per, wanted)
    chosen = (wanted == lane).astype(F32).astype(BF)
    matrix[...] = dot(chosen, table[place]).astype(BF)
    matrix_t[...] = dot_nt(table_t[place], chosen).astype(BF)


def spread_rows(x, table, out, group, mask=None):
    value = x[...]
    for parity in range(2):
        part = value[:, parity * C : (parity + 1) * C]
        for p in range(4):
            result = dot(part, table[p])
            if mask is not None:
                result = result * mask[...]
            out[parity, p] = result.astype(group.dtype)


def fold_rows(parts, table, out, index):
    halves = []
    for parity in range(2):
        total = None
        for p in range(4):
            term = dot(parts[parity, p].astype(BF), table[p])
            total = term if total is None else total + term
        halves.append(total)
    out[index] = jnp.concatenate(halves, axis=1).astype(BF)


def ky_rows(parts, parity, ky2, group):
    rows = pl.ds(pl.multiple_of(ky2 * group.own, group.own), group.own)
    return jnp.concatenate([parts[parity, p, rows, :] for p in range(4)], axis=0).astype(BF)


def set_ky_rows(parts, parity, ky2, group, value):
    rows = pl.ds(pl.multiple_of(ky2 * group.own, group.own), group.own)
    for p in range(4):
        parts[parity, p, rows, :] = value[p * group.own : (p + 1) * group.own].astype(group.dtype)


def spectral_forward(x, w2, spread, gather, mask, l, z, out, index, group):
    spread_rows(x, spread, l, group)

    def body(ky2):
        for parity in range(2):
            value = dot_nt(ky_rows(l, parity, ky2, group), w2[ky2 * 2 + parity])
            set_ky_rows(z, parity, ky2, group, value * mask[0 : 4 * group.own, :])

    loop(0, KY // 2, body, unroll=8)
    fold_rows(z, gather, out, index)


def spectral_backward(d, x, w2, spread, copies, unfold, mask, l, a, z, out, index, group):
    spread_rows(x, spread, l, group)
    spread_rows(d, copies, a, group, mask)

    def body(ky2):
        for parity in range(2):
            value = dot(ky_rows(a, parity, ky2, group), w2[ky2 * 2 + parity])
            set_ky_rows(z, parity, ky2, group, value)

    loop(0, KY // 2, body, unroll=8)
    fold_rows(z, unfold, out, index)


def weight_gradients(a, l, out, groups):
    def body(ky2):
        grads = []
        for parity in range(2):
            left = [ky_rows(a[g], parity, ky2, group) for g, group in enumerate(groups)]
            right = [ky_rows(l[g], parity, ky2, group) for g, group in enumerate(groups)]
            grads.append(dot_tn(jnp.concatenate(left, axis=0), jnp.concatenate(right, axis=0)))
        out[ky2] = jnp.concatenate(grads, axis=1).astype(BF)

    loop(0, KY // 2, body, unroll=4)


def point_sums(ds, a, sums, bias_sum):
    sums[0] += dot_tn(ds[:, :256], a[:, :256])
    sums[1] += dot_tn(ds[:, 128:], a[:, 128:])
    bias_sum[...] += jnp.sum(ds.astype(F32).reshape(-1, 8, PAIR), axis=0)


def fold_point(sums, bias_sum, out):
    total = sums[0][:C, :C] + sums[1][64:, 64:]
    grad = None
    for p in range(4):
        row = total[p * CH : (p + 1) * CH]
        pieces = []
        for b in range(4):
            q = int(np.where(SELECT[p] == b)[0][0])
            piece = row[:, q * CH : (q + 1) * CH]
            pieces.append(piece if SIGNS[p, q] > 0 else -piece)
        term = jnp.concatenate(pieces, axis=1)
        grad = term if grad is None else grad + term
    bias = bias_sum[...]
    bias = jnp.sum(bias[:, :C] + bias[:, C:], axis=0, keepdims=True)
    first = lax.broadcasted_iota(jnp.int32, (16, C), 0) == 0
    for k in range(3):
        out[k, :, 0:C] = grad[k * 16 : (k + 1) * 16]
    out[3, :, 0:C] = jnp.where(first, jnp.broadcast_to(bias, (16, C)), 0.0)


class Refs:
    pass


def main_kernel(names, groups, ranks, *refs):
    r = Refs()
    for name, ref in zip(names, refs, strict=True):
        setattr(r, name, ref)
    reduce_here = ranks == 8
    me = lax.axis_index("modes")
    rank = lax.axis_index("dp")
    core = lax.rem(me, 2)
    chip = me // 2
    mate = (rank, chip * 2 + 1 - core)
    across = (rank, lax.rem(me + 2, 4))

    def mode_device(d):
        return (rank, lax.rem(me + d, 4))

    def rank_device(d):
        return (lax.rem(rank + d, ranks), me)

    def local_copy(source, target, sem):
        copy = pltpu.make_async_copy(source, target, sem)
        copy.start()
        return copy

    def remote(source, target, send, recv, device):
        copy = pltpu.make_async_remote_copy(
            src_ref=source,
            dst_ref=target,
            send_sem=send,
            recv_sem=recv,
            device_id=device,
            device_id_type=pl.DeviceIdType.MESH,
        )
        copy.start()
        return copy

    def per_kind(name):
        return [getattr(r, f"{name}{g.kind}") for g in groups]

    def per_group(name):
        return [getattr(r, f"{name}{g}") for g in range(len(groups))]

    a0, a1, slope, grad, delta = [per_kind(n) for n in ("a0", "a1", "sl", "g", "d")]
    stage, mask, matrix, matrix_t = [per_kind(n) for n in ("stage", "mask", "m", "mt")]
    outs, backs, z = [per_kind(n) for n in ("out", "back", "z")]
    tables = [[getattr(r, f"t{g.kind}{k}") for k in range(4)] for g in groups]
    field, send, recv, out_x, in_x, full, x1, x2, dy, l, a = [
        per_group(n)
        for n in ("field", "send", "recv", "outx", "inx", "full", "x1", "x2", "dy", "l", "a_")
    ]
    bias = [r.bias1, r.bias2]
    points = [(r.pa1, r.pb1), (r.pa2, r.pb2)]
    B1, B2, S1, S2 = range(4)

    loads = [
        local_copy(r.grids1, r.stage1, r.in_sem.at[1]),
        local_copy(r.grids0, r.stage0, r.in_sem.at[0]),
    ][::-1]
    raw_load = local_copy(r.spec1, r.raw, r.in_sem.at[2])

    barrier = pltpu.get_barrier_semaphore()
    for d in range(1, 4):
        pl.semaphore_signal(barrier, inc=1, device_id=mode_device(d), device_id_type=pl.DeviceIdType.MESH)
    if reduce_here:
        for d in range(1, ranks):
            pl.semaphore_signal(barrier, inc=1, device_id=rank_device(d), device_id_type=pl.DeviceIdType.MESH)

    for kind in (1, 0):
        group = groups[2 * kind]
        build_rows(
            r.modes, getattr(r, f"rt{kind}"), getattr(r, f"rtt{kind}"), me,
            getattr(r, f"m{kind}"), getattr(r, f"mt{kind}"), group,
        )
    pl.semaphore_wait(barrier, 3 + (ranks - 1 if reduce_here else 0))

    flights = [{} for _ in groups]

    def hop(g, k, source, target, device):
        flights[g][k] = remote(source, target, r.hops.at[g, k, 0], r.hops.at[g, k, 1], device)

    def start(g):
        send_rows(field[g], matrix[g], send[g], groups[g])
        hop(g, 0, send[g].at[1 - core], recv[g], mate)

    def cross(g):
        if 0 not in flights[g]:
            return
        flights[g].pop(0).wait()
        total = send[g][core, 1 - chip].astype(F32) + recv[g][1 - chip].astype(F32)
        out_x[g][...] = total.astype(BF)
        hop(g, 1, out_x[g], in_x[g], across)

    def land(g, spectral, layer):
        if 1 not in flights[g]:
            return
        flights[g].pop(1).wait()
        total = send[g][core, chip].astype(F32) + recv[g][chip].astype(F32)
        total = (total + in_x[g][...].astype(F32)).astype(BF)
        spectral(g, layer, total)
        hop(g, 2, full[g].at[me], full[g].at[me], across)
        hop(g, 3, full[g].at[me], full[g].at[me], mate)

    def forward(g):
        if 2 not in flights[g]:
            return
        flights[g].pop(2).wait()
        slot = lax.rem(me + 2, 4)
        hop(g, 4, full[g].at[slot], full[g].at[slot], mate)

    def arrive(g):
        flights[g].pop(3).wait()
        flights[g].pop(4).wait()
        receive_rows(field[g], matrix_t[g], full[g], groups[g])

    def spectral(g, layer, total):
        x = (x1, x2)[layer][g]
        x[...] = total
        w2 = (r.w21, r.w22)[layer]
        spectral_forward(x, w2, r.spread, r.gather, mask[g], l[g], z[g], full[g], me, groups[g])

    def spectral_back(g, layer, total):
        x = (x1, x2)[layer][g]
        dy[g][...] = total
        w2 = (r.w21, r.w22)[layer]
        spectral_backward(
            dy[g], x, w2, r.spread, r.copies, r.unfold, mask[g], l[g], a[g], z[g], full[g], me, groups[g]
        )

    writes = []
    dw_copies = {}

    def start_weights(layer):
        out = (r.dw1, r.dw2)[layer]
        weight_gradients(a, l, out, groups)
        if reduce_here:
            dw_copies[layer] = [
                remote(
                    out.at[lax.rem(rank + d, ranks)],
                    (r.dwr1, r.dwr2)[layer].at[d - 1],
                    r.dw_send.at[layer, d - 1],
                    r.dw_recv.at[layer, d - 1],
                    rank_device(d),
                )
                for d in range(1, ranks)
            ]

    def end_weights(layer):
        out = (r.dw1, r.dw2)[layer]
        target = (r.spec_out1, r.spec_out2)[layer]
        if not reduce_here:
            writes.append(local_copy(out, target, r.out_sem.at[layer]))
            return
        for copy in dw_copies[layer]:
            copy.wait()
        total = out[rank].astype(F32)
        for d in range(ranks - 1):
            total = total + (r.dwr1, r.dwr2)[layer][d].astype(F32)
        r.dws[layer] = total
        writes.append(local_copy(r.dws.at[layer], target, r.out_sem.at[layer]))

    point_copies = {}

    def point_first(layer):
        fold_point(r.sums.at[layer], r.bias_sum.at[layer], r.pt_send.at[layer])
        if reduce_here:
            point_copies[layer] = [
                remote(
                    r.pt_send.at[layer, lax.rem(me + d, 4)],
                    r.pt_one.at[layer, d - 1],
                    r.pt_sems.at[layer, 0, d - 1],
                    r.pt_sems.at[layer, 1, d - 1],
                    mode_device(d),
                )
                for d in range(1, 4)
            ]

    def point_second(layer):
        if not reduce_here:
            return
        for copy in point_copies[layer]:
            copy.wait()
        total = r.pt_send[layer, me]
        for d in range(3):
            total = total + r.pt_one[layer, d]
        r.pt_two[layer, rank] = total
        point_copies[layer] = [
            remote(
                r.pt_two.at[layer, rank],
                r.pt_two.at[layer, rank],
                r.pt_sems.at[layer, 2, d - 1],
                r.pt_sems.at[layer, 3, d - 1],
                rank_device(d),
            )
            for d in range(1, ranks)
        ]

    def point_third(layer):
        if not reduce_here:
            return
        for copy in point_copies[layer]:
            copy.wait()
        total = r.pt_two[layer, 0]
        for k in range(1, ranks):
            total = total + r.pt_two[layer, k]
        r.pt_full[layer, me] = total
        point_copies[layer] = [
            remote(
                r.pt_full.at[layer, me],
                r.pt_full.at[layer, me],
                r.pt_sems.at[layer, 4, d - 1],
                r.pt_sems.at[layer, 5, d - 1],
                mode_device(d),
            )
            for d in range(1, 4)
        ]

    def point_last(layer):
        source = r.pt_full if reduce_here else r.pt_send
        if reduce_here:
            for copy in point_copies[layer]:
                copy.wait()
        target = (r.point_out1, r.point_out2)[layer]
        writes.append(local_copy(source.at[layer], target, r.out_sem.at[2 + layer]))

    def first(g):
        group = groups[g]
        pack(stage[g], a0[g], group)

        def body(i):
            analyse(block_of(a0[g], group, i), tables[g][0], field[g], group, i)

        loop(0, group.steps, body)

    def pack_grad(g):
        group = groups[g]
        slot = lax.broadcasted_iota(jnp.int32, (group.count, PAIR), 0) // group.rows
        slot = slot + group.first // group.rows
        count = (r.count0, r.count1)[group.kind][0]
        pack(stage[g], grad[g], group, (slot < count).astype(F32).astype(BF))

    def before_gelu(g, i, x, layer):
        first, second = points[layer]
        linear = pointwise(x, first[...], second[...], dot_nt)
        return synthesise(field[g], tables[g][1], groups[g], i) + linear + bias[layer][...]

    def middle(g, i):
        group = groups[g]
        x = block_of(a0[g], group, i)
        gelu, sl = gelu_and_slope(before_gelu(g, i, x, 0))
        value = (x.astype(F32) + gelu).astype(BF)
        set_block(a1[g], group, i, value)
        set_block(slope[g], group, i, sl.astype(BF))
        analyse(value, tables[g][0], field[g], group, i)

    def turn(g, i):
        group = groups[g]
        x = block_of(a1[g], group, i)
        gelu, sl = gelu_and_slope(before_gelu(g, i, x, 1))
        d = (block_of(grad[g], group, i).astype(F32) * sl).astype(BF)
        set_block(a1[g], group, i, (x.astype(F32) + gelu).astype(BF))
        set_block(delta[g], group, i, d)
        point_sums(d, x, r.sums.at[1], r.bias_sum.at[1])
        analyse(d, tables[g][2], field[g], group, i)

    def gradient(g, i, layer):
        group = groups[g]
        first, second = points[layer]
        linear = pointwise(block_of(delta[g], group, i), first[...], second[...], dot)
        spectral_part = synthesise(field[g], tables[g][3], group, i)
        return spectral_part + linear + block_of(grad[g], group, i).astype(F32)

    def back(g, i):
        group = groups[g]
        g1 = gradient(g, i, 1)
        set_block(grad[g], group, i, g1.astype(BF))
        d = (g1 * block_of(slope[g], group, i).astype(F32)).astype(BF)
        set_block(delta[g], group, i, d)
        point_sums(d, block_of(a0[g], group, i), r.sums.at[0], r.bias_sum.at[0])
        analyse(d, tables[g][2], field[g], group, i)

    def final(g, i):
        set_block(grad[g], groups[g], i, gradient(g, i, 0).astype(BF))

    def write_rows(g, sources, targets, sem):
        rows = pl.ds(groups[g].first, groups[g].count)
        writes.append(local_copy(sources[g].at[rows], targets[g].at[rows], r.row_sem.at[sem, g]))

    def period(step, previous, layer, following, next_layer, after_all=None, middle_hook=None, each=None):
        def done(g):
            if each is not None:
                each(g)
            start(g)

        arrive(S1)
        cross(B2)
        step(S1, 0)
        done(S1)
        land(S2, previous, layer)
        forward(B1)
        arrive(B1)
        cross(S1)
        step(B1, 0)
        land(B2, previous, layer)
        if after_all is not None:
            after_all()
        step(B1, 1)
        done(B1)
        land(S1, following, next_layer)
        forward(S2)
        arrive(S2)
        cross(B1)
        step(S2, 0)
        forward(B2)
        done(S2)
        if middle_hook is not None:
            middle_hook()
        arrive(B2)
        cross(S2)
        step(B2, 0)
        land(B1, following, next_layer)
        forward(S1)
        step(B2, 1)
        done(B2)

    loads[1].wait()
    first(S1)
    start(S1)
    loads[0].wait()
    first(B1)
    cross(S1)
    start(B1)
    first(S2)
    cross(B1)
    start(S2)
    first(B2)
    cross(S2)
    start(B2)
    loads = [local_copy(r.cot0, r.stage0, r.in_sem.at[0]), local_copy(r.cot1, r.stage1, r.in_sem.at[1])]
    raw_load.wait()
    build_weights(r.raw, r.w21)
    raw_load = local_copy(r.spec2, r.raw, r.in_sem.at[2])
    land(S1, spectral, 0)
    cross(B2)
    land(B1, spectral, 0)
    build_point(r.point1, *points[0])
    build_point(r.point2, *points[1])
    r.sums[...] = jnp.zeros_like(r.sums)
    r.bias_sum[...] = jnp.zeros_like(r.bias_sum)
    r.pt_send[...] = jnp.zeros_like(r.pt_send)
    land(S2, spectral, 0)
    loads[1].wait()
    pack_grad(S1)
    pack_grad(S2)
    forward(S1)
    land(B2, spectral, 0)
    loads[0].wait()
    pack_grad(B1)
    forward(B1)
    pack_grad(B2)
    raw_load.wait()
    build_weights(r.raw, r.w22)

    period(middle, spectral, 0, spectral, 1)
    period(turn, spectral, 1, spectral_back, 1, each=lambda g: write_rows(g, a1, outs, 0))
    point_first(1)
    period(
        back, spectral_back, 1, spectral_back, 0,
        after_all=lambda: (point_second(1), start_weights(1)),
        middle_hook=lambda: point_third(1),
    )
    point_first(0)

    def finish_rows(g):
        for i in range(groups[g].steps):
            final(g, i)
        write_rows(g, grad, backs, 1)

    arrive(S1)
    cross(B2)
    finish_rows(S1)
    land(S2, spectral_back, 0)
    forward(B1)
    point_second(0)
    point_last(1)
    land(B2, spectral_back, 0)
    start_weights(0)
    arrive(B1)
    finish_rows(B1)
    forward(S2)
    end_weights(1)
    arrive(S2)
    point_third(0)
    finish_rows(S2)
    forward(B2)
    arrive(B2)
    finish_rows(B2)
    point_last(0)
    end_weights(0)
    for copy in writes:
        copy.wait()


def finish_kernel(*refs, groups, reduce_here):
    refs = list(refs)
    counts = [refs.pop(0) for _ in groups]
    sources = [(refs.pop(0), refs.pop(0)) for _ in groups]
    if reduce_here:
        layers_in = [(refs.pop(0), refs.pop(0)) for _ in range(2)]
    targets = [(refs.pop(0), refs.pop(0)) for _ in groups]
    if reduce_here:
        layers_out = [(refs.pop(0), refs.pop(0), refs.pop(0)) for _ in range(2)]
        lines, flat = refs
    step = pl.program_id(0)
    for group, count, (out_in, back_in), (out, back) in zip(groups, counts, sources, targets):
        row = lax.broadcasted_iota(jnp.int32, (16, PAIR), 0) + step * 16
        live = (row // group.rows < count[0]).astype(F32).astype(BF)
        for source, target, factor in ((out_in, out, live), (back_in, back, None)):
            for first in range(0, group.half, STEP):
                value = jnp.swapaxes(source[:, first : first + STEP, :], 0, 1)
                for j in range(STEP):
                    slab = value[j] if factor is None else value[j] * factor
                    lane = (first + j) * PAIR
                    target[:, lane : lane + PAIR] = slab
    if not reduce_here:
        return
    for k, ((spec_in, point_in), (spec, point, bias)) in enumerate(zip(layers_in, layers_out)):

        @pl.when(step == k)
        def _(spec_in=spec_in, point_in=point_in, spec=spec, point=point, bias=bias):
            for t in range(3):
                lines[t] = spec_in[:, t * 128 : (t + 1) * 128]
            rows = [
                jnp.concatenate([lines[t, pl.ds(o, 24, stride=8), :] for t in range(3)], axis=1)
                for o in range(8)
            ]
            for block in range(8):
                lane = block * CH
                value = jnp.concatenate([v[:, lane : lane + CH] for v in rows], axis=1)
                for t in range(3):
                    flat[t, pl.ds(block * 24, 24), :] = value[:, t * 128 : (t + 1) * 128]
            for block in range(8):
                for high in range(6):
                    for t in range(3):
                        lane = (block * 6 + high) * PAIR + t * 128
                        spec[:, lane : lane + 128] = flat[t, pl.ds(block * 24 + high, 4, stride=6), :]
            for b in range(4):
                for q in range(3):
                    point[b, q * 16 : (q + 1) * 16, :] = point_in[q][:, b * CH : (b + 1) * CH]
            bias[...] = point_in[3][0:1, :C]


def finish(counts, outs, backs, layers, groups, reduce_here):
    def whole(shape):
        return pl.BlockSpec(shape, lambda i: (0,) * len(shape))

    operands, in_specs = list(counts), [pl.BlockSpec(memory_space=pltpu.SMEM)] * len(groups)
    out_specs, out_shape, scratch = [], [], []
    for group, out, back in zip(groups, outs, backs):
        operands += [out, back]
        in_specs += [pl.BlockSpec((16, group.half, PAIR), lambda i: (i, 0, 0))] * 2
        out_specs += [pl.BlockSpec((16, group.width * C), lambda i: (i, 0))] * 2
        out_shape += [struct((group.count, group.width * C))] * 2
    if reduce_here:
        for spec, point in layers:
            operands += [spec, point]
            in_specs += [whole(spec.shape), whole(point.shape)]
            shapes = [(4, C * PAIR // 4), (4, CH, CH), (1, C)]
            out_specs += [whole(s) for s in shapes]
            out_shape += [struct(s, F32) for s in shapes]
        scratch = [pltpu.VMEM((3, C, 128), F32)] * 2
    return pl.pallas_call(
        lambda *refs: finish_kernel(*refs, groups=groups, reduce_here=reduce_here),
        grid=(groups[0].count // 16,),
        in_specs=in_specs,
        out_specs=out_specs,
        out_shape=out_shape,
        scratch_shapes=scratch,
        compiler_params=pltpu.CompilerParams(vmem_limit_bytes=LIMIT),
    )(*operands)


def row_tables(group, parts):
    height = group.rows * parts
    frequency = np.arange(KX)
    frequency = np.where(frequency < KX // 2, frequency, frequency - KX)
    phase = (frequency[:, None] * np.arange(height)[None, :]) % height
    phase = phase.astype(np.float32) * np.float32(2.0 * math.pi / height)
    cosine, sine = np.cos(phase), np.sin(phase)
    both = np.stack([np.stack([cosine, sine], 1), np.stack([-sine, cosine], 1)], 1)
    both = both.reshape(KX, 2, 2, parts, group.rows)
    full = np.zeros((parts, KX, group.slots, 2, 2, group.slots, group.rows), np.float32)
    for s in range(group.slots):
        full[:, :, s, :, :, s, :] = both.transpose(3, 0, 1, 2, 4)
    full = full.reshape(parts, KX * group.slots * 2, 2 * group.count)
    return to_bf(full), to_bf(full.transpose(0, 2, 1))


def local(
    grids_big,
    grids_small,
    counts_big,
    counts_small,
    mode_table,
    spec_one,
    point_one,
    bias_one,
    spec_two,
    point_two,
    bias_two,
    cot_big,
    cot_small,
):
    parts = lax.axis_size("modes")
    ranks = lax.axis_size("dp")
    reduce_here = ranks == 8
    kinds, groups = [], []
    for kind, grids in enumerate((grids_big, grids_small)):
        slots, rows, width = grids.shape[0], grids.shape[1], grids.shape[2] // C
        kinds.append(Group(kind, 0, slots, rows, width, parts))
        for part in range(2):
            groups.append(Group(kind, part * slots * rows // 2, slots // 2, rows, width, parts))
    inputs, outputs, scratch = {}, {}, {}
    smem, vmem, hbm = pltpu.SMEM, pltpu.VMEM, pl.ANY
    inputs["count0"] = (counts_big, smem)
    inputs["count1"] = (counts_small, smem)
    inputs["modes"] = (mode_table, smem)
    arrays = ((grids_big, cot_big), (grids_small, cot_small))
    spread, gather, copies, unfold = blade_tables()
    for k, kind in enumerate(kinds):
        group = groups[2 * k]
        flat = (kind.count, kind.width * C)
        inputs[f"grids{k}"] = (arrays[k][0].reshape(flat), hbm)
        inputs[f"cot{k}"] = (arrays[k][1].reshape(flat), hbm)
        for t, table in enumerate(column_tables(kind.rows * parts, kind.width)):
            inputs[f"t{k}{t}"] = (jnp.asarray(table), vmem)
        straight, turned = row_tables(group, parts)
        inputs[f"rt{k}"] = (jnp.asarray(straight), vmem)
        inputs[f"rtt{k}"] = (jnp.asarray(turned), vmem)
        inputs[f"mask{k}"] = (jnp.asarray(mask_table(group)), vmem)
        scratch[f"m{k}"] = pltpu.VMEM(straight.shape[1:], BF)
        scratch[f"mt{k}"] = pltpu.VMEM(turned.shape[1:], BF)
        rows = (kind.count, kind.half, PAIR)
        outputs[f"out{k}"] = struct(rows)
        outputs[f"back{k}"] = struct(rows)
        scratch[f"stage{k}"] = pltpu.VMEM(flat, BF)
        for name in ("a0", "a1", "sl", "g", "d"):
            scratch[f"{name}{k}"] = pltpu.VMEM(rows, BF)
        scratch[f"z{k}"] = pltpu.VMEM((2, 4, group.lines, C), group.dtype)
    for g, group in enumerate(groups):
        lines = (group.lines, PAIR)
        scratch[f"field{g}"] = pltpu.VMEM((2, group.count * PITCH, 128), F32)
        scratch[f"send{g}"] = pltpu.VMEM((2, 2, *lines), BF)
        scratch[f"recv{g}"] = pltpu.VMEM((2, *lines), BF)
        scratch[f"full{g}"] = pltpu.VMEM((4, *lines), BF)
        for name in ("outx", "inx", "x1", "x2", "dy"):
            scratch[f"{name}{g}"] = pltpu.VMEM(lines, BF)
        for name in ("l", "a_"):
            scratch[f"{name}{g}"] = pltpu.VMEM((2, 4, group.lines, C), group.dtype)
    for name, table in (("spread", spread), ("gather", gather), ("copies", copies), ("unfold", unfold)):
        inputs[name] = (jnp.asarray(table), vmem)
    layers = ((point_one, bias_one, spec_one), (point_two, bias_two, spec_two))
    for k, (point, bias, spec) in enumerate(layers, 1):
        inputs[f"point{k}"] = (point, vmem)
        inputs[f"bias{k}"] = (jnp.concatenate([bias, bias]).reshape(1, PAIR), vmem)
        inputs[f"spec{k}"] = (spec, hbm)
        outputs[f"spec_out{k}"] = struct((C, PAIR), F32) if reduce_here else struct((8, C, PAIR))
        outputs[f"point_out{k}"] = struct((4, 16, 256), F32)
        scratch[f"pa{k}"] = pltpu.VMEM((256, 256), BF)
        scratch[f"pb{k}"] = pltpu.VMEM((256, 256), BF)
        scratch[f"w2{k}"] = pltpu.VMEM((KY, C, C), BF)
        scratch[f"dw{k}"] = pltpu.VMEM((8, C, PAIR), BF)
        if reduce_here:
            scratch[f"dwr{k}"] = pltpu.VMEM((ranks - 1, C, PAIR), BF)
    scratch["raw"] = pltpu.VMEM(spec_one.shape, BF)
    scratch["sums"] = pltpu.VMEM((2, 2, 256, 256), F32)
    scratch["bias_sum"] = pltpu.VMEM((2, 8, PAIR), F32)
    scratch["pt_send"] = pltpu.VMEM((2, 4, 16, 256), F32)
    dma = pltpu.SemaphoreType.DMA
    if reduce_here:
        scratch["dws"] = pltpu.VMEM((2, C, PAIR), F32)
        scratch["pt_one"] = pltpu.VMEM((2, 3, 16, 256), F32)
        scratch["pt_two"] = pltpu.VMEM((2, ranks, 16, 256), F32)
        scratch["pt_full"] = pltpu.VMEM((2, 4, 16, 256), F32)
        scratch["dw_send"] = dma((2, ranks - 1))
        scratch["dw_recv"] = dma((2, ranks - 1))
        scratch["pt_sems"] = dma((2, 6, ranks - 1))
    scratch["hops"] = dma((4, 5, 2))
    scratch["in_sem"] = dma((3,))
    scratch["out_sem"] = dma((4,))
    scratch["row_sem"] = dma((2, 4))
    names = list(inputs) + list(outputs) + list(scratch)
    result = pl.pallas_call(
        lambda *refs: main_kernel(names, groups, ranks, *refs),
        in_specs=[pl.BlockSpec(memory_space=space) for _, space in inputs.values()],
        out_specs=[pl.BlockSpec(memory_space=hbm)] * len(outputs),
        out_shape=list(outputs.values()),
        scratch_shapes=list(scratch.values()),
        compiler_params=pltpu.CompilerParams(
            vmem_limit_bytes=LIMIT, collective_id=0, has_side_effects=True
        ),
    )(*[value for value, _ in inputs.values()])
    result = dict(zip(outputs, result))
    layers = [(result[f"spec_out{k}"], result[f"point_out{k}"]) for k in (1, 2)]
    final = finish(
        (counts_big, counts_small),
        (result["out0"], result["out1"]),
        (result["back0"], result["back1"]),
        layers, kinds, reduce_here,
    )
    out_big, back_big, out_small, back_small = [
        v.reshape(k.slots, k.rows, k.width * C) for v, k in zip(final, (kinds[0],) * 2 + (kinds[1],) * 2)
    ]
    if reduce_here:
        grads = [v.reshape(C) if v.shape == (1, C) else v for v in final[4:]]
        return (out_big, out_small, back_big, back_small, *grads)

    grads = []
    for spec, point in layers:
        spec = spec.reshape(8, 4, CH, 2, 4, CH).transpose(0, 3, 4, 1, 2, 5)
        spec = spec.reshape(ranks, 64 // ranks, 4, CH, CH).astype(F32)
        spec = lax.psum_scatter(spec, "dp", scatter_dimension=0, tiled=False)
        point = lax.psum(point, ("dp", "modes")).reshape(64, 256)
        weight = point[:CH, :C].reshape(CH, 4, CH).transpose(1, 0, 2)
        grads += [spec.transpose(1, 0, 2, 3).reshape(4, -1), weight, point[CH, :C]]
    return (out_big, out_small, back_big, back_small, *grads)


def solution(mesh):
    rows = P("dp", "modes", None)
    spec = P("modes", None, None, None, None)
    return jax.shard_map(
        local,
        mesh=mesh,
        in_specs=(rows, rows, P("dp"), P("dp"), P(), spec, P(), P(), spec, P(), P(), rows, rows),
        out_specs=(rows, rows, rows, rows, P("modes", "dp"), P(), P(), P("modes", "dp"), P(), P()),
        check_vma=False,
    )
```

```python
import math

import jax
import jax.numpy as jnp
import numpy as np
from jax import lax
from jax.experimental import pallas as pl
from jax.experimental.pallas import tpu as pltpu
from jax.sharding import PartitionSpec as P

BF, F32 = jnp.bfloat16, jnp.float32
KX = 16
KY = 16
C = 192
CH = 48
K = 32
PITCH = 40
PAIR = 2 * C
LIMIT = 62 * 2**20
SELECT = np.array([[0, 1, 2, 3], [1, 0, 3, 2], [2, 3, 0, 1], [3, 2, 1, 0]])
SIGNS = np.array(
    [[1.0, 1.0, 1.0, -1.0], [1.0, 1.0, 1.0, -1.0], [1.0, -1.0, 1.0, 1.0], [1.0, -1.0, 1.0, 1.0]]
)


def dot(a, b):
    return jnp.dot(a, b, preferred_element_type=F32)


def dot_nt(a, b):
    return lax.dot_general(a, b, (((1,), (1,)), ((), ())), preferred_element_type=F32)


def dot_tn(a, b):
    return lax.dot_general(a, b, (((0,), (0,)), ((), ())), preferred_element_type=F32)


def to_bf(values):
    return np.asarray(values, np.float32).astype(jnp.bfloat16)


def column_tables(height, width):
    position = np.arange(width)[:, None]
    frequency = np.arange(KY)[None, :]
    phase = ((position * frequency) % width).astype(np.float32) * np.float32(2.0 * math.pi / width)
    col = to_bf(np.stack([np.cos(phase), -np.sin(phase)], -1)).astype(np.float32)
    factor = np.where(np.arange(KY) == 0, 1.0, 2.0) / (height * width)
    inv = to_bf(col * factor[None, :, None].astype(np.float32)).astype(np.float32)
    half = width // 2

    def analysis_form(table):
        return to_bf(table.reshape(half, 2, KY, 2).transpose(3, 2, 1, 0).reshape(K, width))

    def synthesis_form(table):
        return to_bf(table.reshape(half, 2, KY, 2).transpose(0, 1, 3, 2).reshape(half, 2 * K))

    return analysis_form(col), synthesis_form(inv), analysis_form(inv), synthesis_form(col)


def blade_tables():
    eye = np.eye(CH)
    spread = np.zeros((4, C, C))
    gather = np.zeros((4, C, C))
    copies = np.zeros((4, C, C))
    unfold = np.zeros((4, C, C))
    for p in range(4):
        for b in range(4):
            q = int(np.where(SELECT[p] == b)[0][0])
            sign = SIGNS[p, q]
            at_p, at_q, at_b = (slice(i * CH, (i + 1) * CH) for i in (p, q, b))
            spread[p, at_q, at_b] = sign * eye
            unfold[p, at_b, at_q] = sign * eye
            gather[p, at_b, at_p] = eye
            copies[p, at_p, at_b] = eye
    return to_bf(spread), to_bf(gather), to_bf(copies), to_bf(unfold)


def mask_table(group):
    row = np.arange(8 * group.own)[:, None]
    lane = np.arange(C)[None, :]
    return (((row % group.own) // (group.own // 4)) == lane // CH).astype(np.float32)


def analysis(block, table):
    stacked = jnp.concatenate([block[:, :C], block[:, C:]], axis=0)
    return dot(table, stacked)


def put_field(field, n, value):
    field[0, pl.ds(pl.multiple_of(n * PITCH, 8), K), :] = value[:, :128]
    field[1, pl.ds(pl.multiple_of(n * PITCH, 8), K), 0:64] = value[:, 128:]


def get_rows(field, k, count):
    low = field[0, pl.ds(k, count, stride=PITCH), :]
    high = field[1, pl.ds(k, count, stride=PITCH), :]
    return jnp.concatenate([low, high[:, :64]], axis=1).astype(BF)


def rows_forward(field, matrix, ky2, count):
    parts = []
    for parity in range(2):
        ky = ky2 * 2 + parity
        parts.append(
            jnp.concatenate([get_rows(field, ky, count), get_rows(field, KY + ky, count)], axis=0)
        )
    return dot(matrix, jnp.concatenate(parts, axis=1))


def rows_inverse(field, matrix_t, spectrum, ky2, count):
    for parity in range(2):
        value = dot(matrix_t, spectrum[:, parity * C : (parity + 1) * C])
        ky = ky2 * 2 + parity
        for part in range(2):
            piece = value[part * count : (part + 1) * count]
            field[0, pl.ds(part * KY + ky, count, stride=PITCH), :] = piece[:, :128]
            field[1, pl.ds(part * KY + ky, count, stride=PITCH), :] = jnp.concatenate(
                [piece[:, 128:], jnp.zeros((count, 64), F32)], axis=1
            )


def synthesis(field, n, table):
    value = jnp.concatenate(
        [field[0, pl.ds(pl.multiple_of(n * PITCH, 8), K), :], field[1, pl.ds(pl.multiple_of(n * PITCH, 8), K), 0:64]], axis=1
    ).astype(BF)
    zero = jnp.zeros((K, C), BF)
    both = jnp.concatenate(
        [jnp.concatenate([value, zero], axis=1), jnp.concatenate([zero, value], axis=1)], axis=0
    )
    return dot(table, both)


def pointwise(block, first, second, product):
    left = product(block[:, :256], first)
    right = product(block[:, 128:], second)
    return jnp.concatenate(
        [left[:, :128], left[:, 128:] + right[:, :128], right[:, 128:]], axis=1
    )


def gelu_and_slope(value):
    cdf = 0.5 + 0.5 * lax.erf(value * (1.0 / math.sqrt(2.0)))
    bell = jnp.exp(-0.5 * value * value)
    return value * cdf, cdf + value * bell * (1.0 / math.sqrt(2.0 * math.pi))


class Group:
    def __init__(self, kind, first, slots, rows, width, parts):
        self.kind, self.first = kind, first
        self.slots, self.rows, self.width = slots, rows, width
        self.count = slots * rows
        self.half = width // 2
        self.block = 1024 // self.half
        self.steps = self.count // self.block
        self.own = 4 * slots * 2
        self.lines = 8 * self.own
        self.stack = max(1, 16 // self.own)
        self.dtype = F32 if self.own % 16 else BF


def struct(shape, dtype=BF):
    return jax.ShapeDtypeStruct(shape, dtype)


def loop(first, last, body, unroll=1):
    def step(i, carry):
        body(i)
        return carry

    lax.fori_loop(first, last, step, 0, unroll=unroll)


STEP = 16


def pack(source, target, group, live=None):
    rows = slice(group.first, group.first + group.count)
    for first in range(0, group.half, STEP):
        slabs = []
        for j in range(first, first + STEP):
            slab = source[rows, j * PAIR : (j + 1) * PAIR]
            slabs.append(slab if live is None else slab * live)
        target[rows, first : first + STEP, :] = jnp.swapaxes(jnp.stack(slabs, axis=0), 0, 1)


def block_of(ref, group, i):
    rows = pl.ds(group.first + i * group.block, group.block)
    return ref[rows].reshape(group.block * group.half, PAIR)


def set_block(ref, group, i, value):
    rows = pl.ds(group.first + i * group.block, group.block)
    ref[rows] = value.reshape(group.block, group.half, PAIR)


def analyse(value, table, field, group, i):
    t = table[...]
    for q in range(group.block):
        put_field(
            field, i * group.block + q, analysis(value[q * group.half : (q + 1) * group.half], t)
        )


def synthesise(field, table, group, i):
    return jnp.concatenate(
        [synthesis(field, i * group.block + q, table[...]) for q in range(group.block)], axis=0
    )


def send_rows(field, matrix, out, group):
    def body(k):
        values = [
            rows_forward(field, matrix[...], k * group.stack + j, group.count)
            for j in range(group.stack)
        ]
        rows = pl.ds(pl.multiple_of(k * 16, 16), 16)
        for owner in range(4):
            block = slice(owner * group.own, (owner + 1) * group.own)
            piece = jnp.concatenate([v[block] for v in values], axis=0)
            out[owner % 2, owner // 2, rows, :] = piece.astype(BF)

    count = 8 // group.stack
    loop(0, count, body, unroll=count)


def receive_rows(field, matrix_t, spectrum, group):
    def body(k):
        rows = pl.ds(pl.multiple_of(k * 16, 16), 16)
        pieces = [spectrum[owner, rows, :] for owner in range(4)]
        if group.stack > 1:
            pieces = [p.astype(F32) for p in pieces]
        for j in range(group.stack):
            block = slice(j * group.own, (j + 1) * group.own)
            value = jnp.concatenate([p[block] for p in pieces], axis=0).astype(BF)
            rows_inverse(field, matrix_t[...], value, k * group.stack + j, group.count)

    count = 8 // group.stack
    loop(0, count, body, unroll=count)


def build_weights(raw, w2):
    def body(ky):
        parts = [jnp.concatenate([raw[m, ky, b] for m in range(4)], axis=0) for b in range(4)]
        w2[ky] = jnp.concatenate(parts, axis=1)

    loop(0, KY, body, unroll=4)


def build_point(point, first, second):
    rows = []
    for p in range(4):
        pieces = []
        for q in range(4):
            piece = point[int(SELECT[p, q])]
            pieces.append(piece if SIGNS[p, q] > 0 else -piece)
        rows.append(jnp.concatenate(pieces, axis=1))
    matrix = jnp.concatenate(rows, axis=0)
    zero = jnp.zeros((C, C), BF)
    both = jnp.concatenate(
        [jnp.concatenate([matrix, zero], axis=1), jnp.concatenate([zero, matrix], axis=1)], axis=0
    )
    first[...] = both[:256, :256]
    second[...] = both[128:, 128:]
    second[0:128, 0:128] = jnp.zeros((128, 128), BF)


def build_rows(modes, table, table_t, place, matrix, matrix_t, group):
    size = KX * group.slots * 2
    per = group.slots * 2
    row = lax.broadcasted_iota(jnp.int32, (size, size), 0)
    lane = lax.broadcasted_iota(jnp.int32, (size, size), 1)
    wanted = jnp.zeros((size, size), jnp.int32)
    for m in range(KX):
        inside = jnp.logical_and(row >= m * per, row < (m + 1) * per)
        wanted = jnp.where(inside, modes[m] * per + row - m * per, wanted)
    chosen = (wanted == lane).astype(F32).astype(BF)
    matrix[...] = dot(chosen, table[place]).astype(BF)
    matrix_t[...] = dot_nt(table_t[place], chosen).astype(BF)


def spread_rows(value, table, out, group, mask=None):
    for parity in range(2):
        part = value[:, parity * C : (parity + 1) * C]
        for p in range(4):
            result = dot(part, table[p])
            if mask is not None:
                result = result * mask[...]
            out[parity, p] = result.astype(group.dtype)


def fold_rows(parts, table, out, index):
    halves = []
    for parity in range(2):
        total = None
        for p in range(4):
            term = dot(parts[parity, p].astype(BF), table[p])
            total = term if total is None else total + term
        halves.append(total)
    out[index] = jnp.concatenate(halves, axis=1).astype(BF)


def ky_rows(parts, parity, ky2, group):
    rows = pl.ds(pl.multiple_of(ky2 * group.own, group.own), group.own)
    return jnp.concatenate([parts[parity, p, rows, :] for p in range(4)], axis=0).astype(BF)


def set_ky_rows(parts, parity, ky2, group, value):
    rows = pl.ds(pl.multiple_of(ky2 * group.own, group.own), group.own)
    for p in range(4):
        parts[parity, p, rows, :] = value[p * group.own : (p + 1) * group.own].astype(group.dtype)


def spectral_forward(x, w2, spread, gather, mask, l, z, out, index, group):
    spread_rows(x, spread, l, group)

    def body(ky2):
        for parity in range(2):
            value = dot_nt(ky_rows(l, parity, ky2, group), w2[ky2 * 2 + parity])
            set_ky_rows(z, parity, ky2, group, value * mask[0 : 4 * group.own, :])

    loop(0, KY // 2, body, unroll=8)
    fold_rows(z, gather, out, index)


def spectral_backward(d, w2, copies, unfold, mask, a, z, out, index, group):
    spread_rows(d, copies, a, group, mask)

    def body(ky2):
        for parity in range(2):
            value = dot(ky_rows(a, parity, ky2, group), w2[ky2 * 2 + parity])
            set_ky_rows(z, parity, ky2, group, value)

    loop(0, KY // 2, body, unroll=8)
    fold_rows(z, unfold, out, index)


def weight_gradient(x, d, spread, copies, mask):
    halves = []
    for parity in range(2):
        lanes = slice(parity * C, (parity + 1) * C)
        total = None
        for p in range(4):
            right = dot(x[:, lanes], spread[p]).astype(BF)
            left = (dot(d[:, lanes], copies[p]) * mask[...]).astype(BF)
            term = dot_tn(left, right)
            total = term if total is None else total + term
        halves.append(total)
    return jnp.concatenate(halves, axis=1)


def point_sums(ds, a, sums, bias_sum):
    sums[0] += dot_tn(ds[:, :256], a[:, :256])
    sums[1] += dot_tn(ds[:, 128:], a[:, 128:])
    bias_sum[...] += jnp.sum(ds.astype(F32).reshape(-1, 8, PAIR), axis=0)


def fold_point(sums, bias_sum, out):
    total = sums[0][:C, :C] + sums[1][64:, 64:]
    grad = None
    for p in range(4):
        row = total[p * CH : (p + 1) * CH]
        pieces = []
        for b in range(4):
            q = int(np.where(SELECT[p] == b)[0][0])
            piece = row[:, q * CH : (q + 1) * CH]
            pieces.append(piece if SIGNS[p, q] > 0 else -piece)
        term = jnp.concatenate(pieces, axis=1)
        grad = term if grad is None else grad + term
    bias = bias_sum[...]
    bias = jnp.sum(bias[:, :C] + bias[:, C:], axis=0, keepdims=True)
    first = lax.broadcasted_iota(jnp.int32, (16, C), 0) == 0
    for k in range(3):
        out[k, :, 0:C] = grad[k * 16 : (k + 1) * 16]
    out[3, :, 0:C] = jnp.where(first, jnp.broadcast_to(bias, (16, C)), 0.0)


class Refs:
    pass


def main_kernel(names, groups, ranks, *refs):
    r = Refs()
    for name, ref in zip(names, refs, strict=True):
        setattr(r, name, ref)
    reduce_here = ranks == 8
    me = lax.axis_index("modes")
    rank = lax.axis_index("dp")
    core = lax.rem(me, 2)
    chip = me // 2
    mate = (rank, chip * 2 + 1 - core)
    across = (rank, lax.rem(me + 2, 4))

    def mode_device(d):
        return (rank, lax.rem(me + d, 4))

    def rank_device(d):
        return (lax.rem(rank + d, ranks), me)

    def local_copy(source, target, sem):
        copy = pltpu.make_async_copy(source, target, sem)
        copy.start()
        return copy

    def remote(source, target, send, recv, device):
        copy = pltpu.make_async_remote_copy(
            src_ref=source,
            dst_ref=target,
            send_sem=send,
            recv_sem=recv,
            device_id=device,
            device_id_type=pl.DeviceIdType.MESH,
        )
        copy.start()
        return copy

    def per_kind(name):
        return [getattr(r, f"{name}{g.kind}") for g in groups]

    def per_group(name):
        return [getattr(r, f"{name}{g}") for g in range(len(groups))]

    a0, a1, slope, grad, delta = [per_kind(n) for n in ("a0", "a1", "sl", "g", "d")]
    stage, mask, matrix, matrix_t = [per_kind(n) for n in ("stage", "mask", "m", "mt")]
    outs, backs, l, z = [per_kind(n) for n in ("out", "back", "l", "z")]
    tables = [[getattr(r, f"t{g.kind}{k}") for k in range(4)] for g in groups]
    field, send, recv, out_x, in_x, full = [
        per_group(n) for n in ("field", "send", "recv", "outx", "inx", "full")
    ]
    points = [(r.pa1, r.pb1), (r.pa2, r.pb2)]
    B1, B2, S1, S2 = range(4)

    loads = [
        local_copy(r.grids1, r.stage1, r.in_sem.at[1]),
        local_copy(r.grids0, r.stage0, r.in_sem.at[0]),
    ][::-1]
    raw_load = local_copy(r.spec1, r.raw, r.in_sem.at[2])

    barrier = pltpu.get_barrier_semaphore()
    for d in range(1, 4):
        pl.semaphore_signal(barrier, inc=1, device_id=mode_device(d), device_id_type=pl.DeviceIdType.MESH)
    if reduce_here:
        for d in range(1, ranks):
            pl.semaphore_signal(barrier, inc=1, device_id=rank_device(d), device_id_type=pl.DeviceIdType.MESH)

    for kind in (1, 0):
        group = groups[2 * kind]
        build_rows(
            r.modes, getattr(r, f"rt{kind}"), getattr(r, f"rtt{kind}"), me,
            getattr(r, f"m{kind}"), getattr(r, f"mt{kind}"), group,
        )
    pl.semaphore_wait(barrier, 3 + (ranks - 1 if reduce_here else 0))

    flights = [{} for _ in groups]

    def hop(g, k, source, target, device):
        flights[g][k] = remote(source, target, r.hops.at[g, k, 0], r.hops.at[g, k, 1], device)

    def start(g):
        send_rows(field[g], matrix[g], send[g], groups[g])
        hop(g, 0, send[g].at[1 - core], recv[g], mate)

    def cross(g):
        if 0 not in flights[g]:
            return
        flights[g].pop(0).wait()
        total = send[g][core, 1 - chip].astype(F32) + recv[g][1 - chip].astype(F32)
        out_x[g][...] = total.astype(BF)
        hop(g, 1, out_x[g], in_x[g], across)

    def land(g, spectral, layer):
        if 1 not in flights[g]:
            return
        flights[g].pop(1).wait()
        total = send[g][core, chip].astype(F32) + recv[g][chip].astype(F32)
        total = total + in_x[g][...].astype(F32)
        spectral(g, layer, total)
        hop(g, 2, full[g].at[me], full[g].at[me], across)
        hop(g, 3, full[g].at[me], full[g].at[me], mate)

    def forward(g):
        if 2 not in flights[g]:
            return
        flights[g].pop(2).wait()
        slot = lax.rem(me + 2, 4)
        hop(g, 4, full[g].at[slot], full[g].at[slot], mate)

    def arrive(g):
        flights[g].pop(3).wait()
        flights[g].pop(4).wait()
        receive_rows(field[g], matrix_t[g], full[g], groups[g])

    def keep(g, layer, which, total):
        group = groups[g]
        rows = slice(group.keep, group.keep + group.own)
        r.factors[layer, which, :, rows, :] = total.reshape(8, group.own, PAIR).astype(BF)

    def spectral(g, layer, total):
        keep(g, layer, 0, total)
        w2 = (r.w21, r.w22)[layer]
        spectral_forward(
            total.astype(BF), w2, r.spread, r.gather, mask[g], l[g], z[g], full[g], me, groups[g]
        )

    def spectral_back(g, layer, total):
        keep(g, layer, 1, total)
        w2 = (r.w21, r.w22)[layer]
        spectral_backward(
            total.astype(BF), w2, r.copies, r.unfold, mask[g], l[g], z[g], full[g], me, groups[g]
        )

    writes = []
    factor_copies = {}

    def start_factors(layer, which):
        if not reduce_here:
            return
        factor_copies[layer, which] = [
            remote(
                r.factors.at[layer, which, lax.rem(rank + d, ranks)],
                r.factors_in.at[layer, which, d],
                r.dw_send.at[layer, which, d - 1],
                r.dw_recv.at[layer, which, d - 1],
                rank_device(d),
            )
            for d in range(1, ranks)
        ]

    def end_factors(layer):
        target = (r.spec_out1, r.spec_out2)[layer]
        if not reduce_here:
            mask_rows = r.keep_mask[...]

            def body(ky2):
                r.dws[ky2] = weight_gradient(
                    r.factors[layer, 0, ky2], r.factors[layer, 1, ky2], r.spread, r.copies, mask_rows
                ).astype(BF)

            loop(0, 8, body)
            copy = local_copy(r.dws, target, r.out_sem.at[layer])
            copy.wait()
            return
        values = []
        for which in range(2):
            for copy in factor_copies[layer, which]:
                copy.wait()
            pieces = [r.factors[layer, which, rank]]
            pieces += [r.factors_in[layer, which, d] for d in range(1, ranks)]
            values.append(jnp.concatenate(pieces, axis=0))
        mask_rows = jnp.concatenate([r.keep_mask[...]] * ranks, axis=0)
        r.dws[layer] = weight_gradient(*values, r.spread, r.copies, mask_rows)
        writes.append(local_copy(r.dws.at[layer], target, r.out_sem.at[layer]))

    point_copies = {}

    def point_first(layer):
        fold_point(r.sums.at[layer], r.bias_sum.at[layer], r.pt_send.at[layer])
        if reduce_here:
            point_copies[layer] = [
                remote(
                    r.pt_send.at[layer, lax.rem(me + d, 4)],
                    r.pt_one.at[layer, d - 1],
                    r.pt_sems.at[layer, 0, d - 1],
                    r.pt_sems.at[layer, 1, d - 1],
                    mode_device(d),
                )
                for d in range(1, 4)
            ]

    def point_second(layer):
        if not reduce_here:
            return
        for copy in point_copies[layer]:
            copy.wait()
        total = r.pt_send[layer, me]
        for d in range(3):
            total = total + r.pt_one[layer, d]
        r.pt_two[layer, rank] = total
        point_copies[layer] = [
            remote(
                r.pt_two.at[layer, rank],
                r.pt_two.at[layer, rank],
                r.pt_sems.at[layer, 2, d - 1],
                r.pt_sems.at[layer, 3, d - 1],
                rank_device(d),
            )
            for d in range(1, ranks)
        ]

    def point_third(layer):
        if not reduce_here:
            return
        for copy in point_copies[layer]:
            copy.wait()
        total = r.pt_two[layer, 0]
        for k in range(1, ranks):
            total = total + r.pt_two[layer, k]
        r.pt_full[layer, me] = total
        point_copies[layer] = [
            remote(
                r.pt_full.at[layer, me],
                r.pt_full.at[layer, me],
                r.pt_sems.at[layer, 4, d - 1],
                r.pt_sems.at[layer, 5, d - 1],
                mode_device(d),
            )
            for d in range(1, 4)
        ]

    def point_last(layer):
        source = r.pt_full if reduce_here else r.pt_send
        if reduce_here:
            for copy in point_copies[layer]:
                copy.wait()
        target = (r.point_out1, r.point_out2)[layer]
        writes.append(local_copy(source.at[layer], target, r.out_sem.at[2 + layer]))

    def first(g):
        group = groups[g]
        pack(stage[g], a0[g], group)

        def body(i):
            analyse(block_of(a0[g], group, i), tables[g][0], field[g], group, i)

        loop(0, group.steps, body)

    def pack_grad(g):
        group = groups[g]
        slot = lax.broadcasted_iota(jnp.int32, (group.count, PAIR), 0) // group.rows
        slot = slot + group.first // group.rows
        count = (r.count0, r.count1)[group.kind][0]
        pack(stage[g], grad[g], group, (slot < count).astype(F32).astype(BF))

    def before_gelu(g, i, x, layer):
        first, second = points[layer]
        linear = pointwise(x, first[...], second[...], dot_nt)
        return synthesise(field[g], tables[g][1], groups[g], i) + linear + r.bias_pair[layer]

    def middle(g, i):
        group = groups[g]
        x = block_of(a0[g], group, i)
        gelu, sl = gelu_and_slope(before_gelu(g, i, x, 0))
        value = (x.astype(F32) + gelu).astype(BF)
        set_block(a1[g], group, i, value)
        set_block(slope[g], group, i, sl.astype(BF))
        analyse(value, tables[g][0], field[g], group, i)

    def turn(g, i):
        group = groups[g]
        x = block_of(a1[g], group, i)
        gelu, sl = gelu_and_slope(before_gelu(g, i, x, 1))
        d = (block_of(grad[g], group, i).astype(F32) * sl).astype(BF)
        set_block(a1[g], group, i, (x.astype(F32) + gelu).astype(BF))
        set_block(delta[g], group, i, d)
        point_sums(d, x, r.sums.at[1], r.bias_sum.at[1])
        analyse(d, tables[g][2], field[g], group, i)

    def gradient(g, i, layer):
        group = groups[g]
        first, second = points[layer]
        linear = pointwise(block_of(delta[g], group, i), first[...], second[...], dot)
        spectral_part = synthesise(field[g], tables[g][3], group, i)
        return spectral_part + linear + block_of(grad[g], group, i).astype(F32)

    def back(g, i):
        group = groups[g]
        g1 = gradient(g, i, 1)
        set_block(grad[g], group, i, g1.astype(BF))
        d = (g1 * block_of(slope[g], group, i).astype(F32)).astype(BF)
        set_block(delta[g], group, i, d)
        point_sums(d, block_of(a0[g], group, i), r.sums.at[0], r.bias_sum.at[0])
        analyse(d, tables[g][2], field[g], group, i)

    def final(g, i):
        set_block(grad[g], groups[g], i, gradient(g, i, 0).astype(BF))

    def write_rows(g, sources, targets, sem):
        rows = pl.ds(groups[g].first, groups[g].count)
        writes.append(local_copy(sources[g].at[rows], targets[g].at[rows], r.row_sem.at[sem, g]))

    def period(step, previous, layer, following, next_layer, after_all=None, each=None):
        def done(g):
            if each is not None:
                each(g)
            start(g)

        arrive(S1)
        forward(B1)
        step(S1, 0)
        cross(B2)
        done(S1)
        land(S2, previous, layer)
        arrive(B1)
        cross(S1)
        step(B1, 0)
        land(B2, previous, layer)
        if after_all is not None:
            after_all()
        step(B1, 1)
        forward(S2)
        done(B1)
        land(S1, following, next_layer)
        arrive(S2)
        cross(B1)
        forward(B2)
        step(S2, 0)
        done(S2)
        arrive(B2)
        step(B2, 0)
        cross(S2)
        land(B1, following, next_layer)
        forward(S1)
        step(B2, 1)
        done(B2)

    loads[1].wait()
    first(S1)
    start(S1)
    loads[0].wait()
    first(B1)
    cross(S1)
    start(B1)
    first(S2)
    cross(B1)
    start(S2)
    first(B2)
    cross(S2)
    start(B2)
    loads = [local_copy(r.cot0, r.stage0, r.in_sem.at[0]), local_copy(r.cot1, r.stage1, r.in_sem.at[1])]
    raw_load.wait()
    build_weights(r.raw, r.w21)
    raw_load = local_copy(r.spec2, r.raw, r.in_sem.at[2])
    land(S1, spectral, 0)
    cross(B2)
    land(B1, spectral, 0)
    for k, value in enumerate((r.bias1, r.bias2)):
        row = value[...].reshape(1, C)
        r.bias_pair[k] = jnp.concatenate([row, row], axis=1)
    build_point(r.point1, *points[0])
    build_point(r.point2, *points[1])
    r.sums[...] = jnp.zeros_like(r.sums)
    r.bias_sum[...] = jnp.zeros_like(r.bias_sum)
    r.pt_send[...] = jnp.zeros_like(r.pt_send)
    land(S2, spectral, 0)
    loads[1].wait()
    pack_grad(S1)
    pack_grad(S2)
    forward(S1)
    land(B2, spectral, 0)
    loads[0].wait()
    pack_grad(B1)
    forward(B1)
    pack_grad(B2)
    raw_load.wait()
    build_weights(r.raw, r.w22)

    start_factors(0, 0)

    period(middle, spectral, 0, spectral, 1)
    period(
        turn, spectral, 1, spectral_back, 1,
        after_all=lambda: start_factors(1, 0),
        each=lambda g: write_rows(g, a1, outs, 0),
    )
    point_first(1)
    period(
        back, spectral_back, 1, spectral_back, 0,
        after_all=lambda: (point_second(1), start_factors(1, 1)),
    )
    point_first(0)

    def finish_rows(g):
        for i in range(groups[g].steps):
            final(g, i)
        write_rows(g, grad, backs, 1)

    arrive(S1)
    forward(B1)
    finish_rows(S1)
    cross(B2)
    point_third(1)
    point_second(0)
    land(S2, spectral_back, 0)
    arrive(B1)
    end_factors(1)
    land(B2, spectral_back, 0)
    start_factors(0, 1)
    finish_rows(B1)
    forward(S2)
    forward(B2)
    point_last(1)
    point_third(0)
    arrive(S2)
    finish_rows(S2)
    end_factors(0)
    arrive(B2)
    finish_rows(B2)
    point_last(0)
    for copy in writes:
        copy.wait()


def finish_kernel(*refs, groups, reduce_here):
    refs = list(refs)
    counts = [refs.pop(0) for _ in groups]
    sources = [(refs.pop(0), refs.pop(0)) for _ in groups]
    if reduce_here:
        layers_in = [(refs.pop(0), refs.pop(0)) for _ in range(2)]
    targets = [(refs.pop(0), refs.pop(0)) for _ in groups]
    if reduce_here:
        layers_out = [(refs.pop(0), refs.pop(0), refs.pop(0)) for _ in range(2)]
        lines, flat = refs
    step = pl.program_id(0)
    for group, count, (out_in, back_in), (out, back) in zip(groups, counts, sources, targets):
        row = lax.broadcasted_iota(jnp.int32, (16, PAIR), 0) + step * 16
        live = (row // group.rows < count[0]).astype(F32).astype(BF)
        for source, target, factor in ((out_in, out, live), (back_in, back, None)):
            for first in range(0, group.half, STEP):
                value = jnp.swapaxes(source[:, first : first + STEP, :], 0, 1)
                for j in range(STEP):
                    slab = value[j] if factor is None else value[j] * factor
                    lane = (first + j) * PAIR
                    target[:, lane : lane + PAIR] = slab
    if not reduce_here:
        return
    for k, ((spec_in, point_in), (spec, point, bias)) in enumerate(zip(layers_in, layers_out)):

        @pl.when(step == k)
        def _(spec_in=spec_in, point_in=point_in, spec=spec, point=point, bias=bias):
            for t in range(3):
                lines[t] = spec_in[:, t * 128 : (t + 1) * 128]
            rows = [
                jnp.concatenate([lines[t, pl.ds(o, 24, stride=8), :] for t in range(3)], axis=1)
                for o in range(8)
            ]
            for block in range(8):
                lane = block * CH
                value = jnp.concatenate([v[:, lane : lane + CH] for v in rows], axis=1)
                for t in range(3):
                    flat[t, pl.ds(block * 24, 24), :] = value[:, t * 128 : (t + 1) * 128]
            for block in range(8):
                for high in range(6):
                    for t in range(3):
                        lane = (block * 6 + high) * PAIR + t * 128
                        spec[:, lane : lane + 128] = flat[t, pl.ds(block * 24 + high, 4, stride=6), :]
            for b in range(4):
                for q in range(3):
                    point[b, q * 16 : (q + 1) * 16, :] = point_in[q][:, b * CH : (b + 1) * CH]
            bias[...] = point_in[3][0:1, :C]


def finish(counts, outs, backs, layers, groups, reduce_here):
    def whole(shape):
        return pl.BlockSpec(shape, lambda i: (0,) * len(shape))

    operands, in_specs = list(counts), [pl.BlockSpec(memory_space=pltpu.SMEM)] * len(groups)
    out_specs, out_shape, scratch = [], [], []
    for group, out, back in zip(groups, outs, backs):
        operands += [out, back]
        in_specs += [pl.BlockSpec((16, group.half, PAIR), lambda i: (i, 0, 0))] * 2
        out_specs += [pl.BlockSpec((16, group.width * C), lambda i: (i, 0))] * 2
        out_shape += [struct((group.count, group.width * C))] * 2
    if reduce_here:
        for spec, point in layers:
            operands += [spec, point]
            in_specs += [whole(spec.shape), whole(point.shape)]
            shapes = [(4, C * PAIR // 4), (4, CH, CH), (1, C)]
            out_specs += [whole(s) for s in shapes]
            out_shape += [struct(s, F32) for s in shapes]
        scratch = [pltpu.VMEM((3, C, 128), F32)] * 2
    return pl.pallas_call(
        lambda *refs: finish_kernel(*refs, groups=groups, reduce_here=reduce_here),
        grid=(groups[0].count // 16,),
        in_specs=in_specs,
        out_specs=out_specs,
        out_shape=out_shape,
        scratch_shapes=scratch,
        compiler_params=pltpu.CompilerParams(vmem_limit_bytes=LIMIT),
    )(*operands)


def row_tables(group, parts):
    height = group.rows * parts
    frequency = np.arange(KX)
    frequency = np.where(frequency < KX // 2, frequency, frequency - KX)
    phase = (frequency[:, None] * np.arange(height)[None, :]) % height
    phase = phase.astype(np.float32) * np.float32(2.0 * math.pi / height)
    cosine, sine = np.cos(phase), np.sin(phase)
    both = np.stack([np.stack([cosine, sine], 1), np.stack([-sine, cosine], 1)], 1)
    both = both.reshape(KX, 2, 2, parts, group.rows)
    full = np.zeros((parts, KX, group.slots, 2, 2, group.slots, group.rows), np.float32)
    for s in range(group.slots):
        full[:, :, s, :, :, s, :] = both.transpose(3, 0, 1, 2, 4)
    full = full.reshape(parts, KX * group.slots * 2, 2 * group.count)
    return to_bf(full), to_bf(full.transpose(0, 2, 1))


def local(
    grids_big,
    grids_small,
    counts_big,
    counts_small,
    mode_table,
    spec_one,
    point_one,
    bias_one,
    spec_two,
    point_two,
    bias_two,
    cot_big,
    cot_small,
):
    parts = lax.axis_size("modes")
    ranks = lax.axis_size("dp")
    reduce_here = ranks == 8
    kinds, groups = [], []
    for kind, grids in enumerate((grids_big, grids_small)):
        slots, rows, width = grids.shape[0], grids.shape[1], grids.shape[2] // C
        kinds.append(Group(kind, 0, slots, rows, width, parts))
        for part in range(2):
            groups.append(Group(kind, part * slots * rows // 2, slots // 2, rows, width, parts))
    total_rows = 0
    for group in groups[2:] + groups[:2]:
        group.keep = total_rows
        total_rows += group.own
    inputs, outputs, scratch = {}, {}, {}
    smem, vmem, hbm = pltpu.SMEM, pltpu.VMEM, pl.ANY
    inputs["count0"] = (counts_big, smem)
    inputs["count1"] = (counts_small, smem)
    inputs["modes"] = (mode_table, smem)
    arrays = ((grids_big, cot_big), (grids_small, cot_small))
    spread, gather, copies, unfold = blade_tables()
    for k, kind in enumerate(kinds):
        group = groups[2 * k]
        flat = (kind.count, kind.width * C)
        inputs[f"grids{k}"] = (arrays[k][0].reshape(flat), hbm)
        inputs[f"cot{k}"] = (arrays[k][1].reshape(flat), hbm)
        for t, table in enumerate(column_tables(kind.rows * parts, kind.width)):
            inputs[f"t{k}{t}"] = (jnp.asarray(table), vmem)
        straight, turned = row_tables(group, parts)
        inputs[f"rt{k}"] = (jnp.asarray(straight), vmem)
        inputs[f"rtt{k}"] = (jnp.asarray(turned), vmem)
        inputs[f"mask{k}"] = (jnp.asarray(mask_table(group)), vmem)
        scratch[f"m{k}"] = pltpu.VMEM(straight.shape[1:], BF)
        scratch[f"mt{k}"] = pltpu.VMEM(turned.shape[1:], BF)
        rows = (kind.count, kind.half, PAIR)
        outputs[f"out{k}"] = struct(rows)
        outputs[f"back{k}"] = struct(rows)
        scratch[f"stage{k}"] = pltpu.VMEM(flat, BF)
        for name in ("a0", "a1", "sl", "g", "d"):
            scratch[f"{name}{k}"] = pltpu.VMEM(rows, BF)
        for name in ("l", "z"):
            scratch[f"{name}{k}"] = pltpu.VMEM((2, 4, group.lines, C), group.dtype)
    for g, group in enumerate(groups):
        lines = (group.lines, PAIR)
        scratch[f"field{g}"] = pltpu.VMEM((2, group.count * PITCH, 128), F32)
        scratch[f"send{g}"] = pltpu.VMEM((2, 2, *lines), BF)
        scratch[f"recv{g}"] = pltpu.VMEM((2, *lines), BF)
        scratch[f"full{g}"] = pltpu.VMEM((4, *lines), BF)
        for name in ("outx", "inx"):
            scratch[f"{name}{g}"] = pltpu.VMEM(lines, BF)
    for name, table in (("spread", spread), ("gather", gather), ("copies", copies), ("unfold", unfold)):
        inputs[name] = (jnp.asarray(table), vmem)
    keep_mask = np.concatenate([mask_table(g)[: g.own] for g in groups[2:] + groups[:2]])
    inputs["keep_mask"] = (jnp.asarray(keep_mask), vmem)
    layers = ((point_one, bias_one, spec_one), (point_two, bias_two, spec_two))
    for k, (point, bias, spec) in enumerate(layers, 1):
        inputs[f"point{k}"] = (point, vmem)
        inputs[f"bias{k}"] = (bias, vmem)
        inputs[f"spec{k}"] = (spec, hbm)
        outputs[f"spec_out{k}"] = struct((C, PAIR), F32) if reduce_here else struct((8, C, PAIR))
        outputs[f"point_out{k}"] = struct((4, 16, 256), F32)
        scratch[f"pa{k}"] = pltpu.VMEM((256, 256), BF)
        scratch[f"pb{k}"] = pltpu.VMEM((256, 256), BF)
        scratch[f"w2{k}"] = pltpu.VMEM((KY, C, C), BF)
    scratch["raw"] = pltpu.VMEM(spec_one.shape, BF)
    scratch["bias_pair"] = pltpu.VMEM((2, 1, PAIR), F32)
    scratch["sums"] = pltpu.VMEM((2, 2, 256, 256), F32)
    scratch["bias_sum"] = pltpu.VMEM((2, 8, PAIR), F32)
    scratch["pt_send"] = pltpu.VMEM((2, 4, 16, 256), F32)
    dma = pltpu.SemaphoreType.DMA
    if reduce_here:
        scratch["factors_in"] = pltpu.VMEM((2, 2, ranks, total_rows, PAIR), BF)
        scratch["dws"] = pltpu.VMEM((2, C, PAIR), F32)
        scratch["pt_one"] = pltpu.VMEM((2, 3, 16, 256), F32)
        scratch["pt_two"] = pltpu.VMEM((2, ranks, 16, 256), F32)
        scratch["pt_full"] = pltpu.VMEM((2, 4, 16, 256), F32)
        scratch["dw_send"] = dma((2, 2, ranks - 1))
        scratch["dw_recv"] = dma((2, 2, ranks - 1))
        scratch["pt_sems"] = dma((2, 6, ranks - 1))
    else:
        scratch["dws"] = pltpu.VMEM((8, C, PAIR), BF)
    scratch["factors"] = pltpu.VMEM((2, 2, 8, total_rows, PAIR), BF)
    scratch["hops"] = dma((4, 5, 2))
    scratch["in_sem"] = dma((3,))
    scratch["out_sem"] = dma((4,))
    scratch["row_sem"] = dma((2, 4))
    names = list(inputs) + list(outputs) + list(scratch)
    result = pl.pallas_call(
        lambda *refs: main_kernel(names, groups, ranks, *refs),
        in_specs=[pl.BlockSpec(memory_space=space) for _, space in inputs.values()],
        out_specs=[pl.BlockSpec(memory_space=hbm)] * len(outputs),
        out_shape=list(outputs.values()),
        scratch_shapes=list(scratch.values()),
        compiler_params=pltpu.CompilerParams(
            vmem_limit_bytes=LIMIT, collective_id=0, has_side_effects=True
        ),
    )(*[value for value, _ in inputs.values()])
    result = dict(zip(outputs, result))
    layers = [(result[f"spec_out{k}"], result[f"point_out{k}"]) for k in (1, 2)]
    final = finish(
        (counts_big, counts_small),
        (result["out0"], result["out1"]),
        (result["back0"], result["back1"]),
        layers, kinds, reduce_here,
    )
    out_big, back_big, out_small, back_small = [
        v.reshape(k.slots, k.rows, k.width * C) for v, k in zip(final, (kinds[0],) * 2 + (kinds[1],) * 2)
    ]
    if reduce_here:
        grads = [v.reshape(C) if v.shape == (1, C) else v for v in final[4:]]
        return (out_big, out_small, back_big, back_small, *grads)

    grads = []
    for spec, point in layers:
        spec = spec.reshape(8, 4, CH, 2, 4, CH).transpose(0, 3, 4, 1, 2, 5)
        spec = spec.reshape(ranks, 64 // ranks, 4, CH, CH).astype(F32)
        spec = lax.psum_scatter(spec, "dp", scatter_dimension=0, tiled=False)
        point = lax.psum(point, ("dp", "modes")).reshape(64, 256)
        weight = point[:CH, :C].reshape(CH, 4, CH).transpose(1, 0, 2)
        grads += [spec.transpose(1, 0, 2, 3).reshape(4, -1), weight, point[CH, :C]]
    return (out_big, out_small, back_big, back_small, *grads)


def solution(mesh):
    rows = P("dp", "modes", None)
    spec = P("modes", None, None, None, None)
    return jax.shard_map(
        local,
        mesh=mesh,
        in_specs=(rows, rows, P("dp"), P("dp"), P(), spec, P(), P(), spec, P(), P(), rows, rows),
        out_specs=(rows, rows, rows, rows, P("modes", "dp"), P(), P(), P("modes", "dp"), P(), P()),
        check_vma=False,
    )
```

```python
import math

import jax
import jax.numpy as jnp
import numpy as np
from jax import lax
from jax.experimental import pallas as pl
from jax.experimental.pallas import tpu as pltpu
from jax.sharding import PartitionSpec as P

BF, F32 = jnp.bfloat16, jnp.float32
KX = 16
KY = 16
C = 192
CH = 48
K = 32
PITCH = 40
PAIR = 2 * C
LIMIT = 62 * 2**20
SELECT = np.array([[0, 1, 2, 3], [1, 0, 3, 2], [2, 3, 0, 1], [3, 2, 1, 0]])
SIGNS = np.array(
    [[1.0, 1.0, 1.0, -1.0], [1.0, 1.0, 1.0, -1.0], [1.0, -1.0, 1.0, 1.0], [1.0, -1.0, 1.0, 1.0]]
)


def dot(a, b):
    return jnp.dot(a, b, preferred_element_type=F32)


def dot_nt(a, b):
    return lax.dot_general(a, b, (((1,), (1,)), ((), ())), preferred_element_type=F32)


def dot_tn(a, b):
    return lax.dot_general(a, b, (((0,), (0,)), ((), ())), preferred_element_type=F32)


def to_bf(values):
    return np.asarray(values, np.float32).astype(jnp.bfloat16)


def column_tables(height, width):
    position = np.arange(width)[:, None]
    frequency = np.arange(KY)[None, :]
    phase = ((position * frequency) % width).astype(np.float32) * np.float32(2.0 * math.pi / width)
    col = to_bf(np.stack([np.cos(phase), -np.sin(phase)], -1)).astype(np.float32)
    factor = np.where(np.arange(KY) == 0, 1.0, 2.0) / (height * width)
    inv = to_bf(col * factor[None, :, None].astype(np.float32)).astype(np.float32)
    half = width // 2

    def analysis_form(table):
        return to_bf(table.reshape(half, 2, KY, 2).transpose(3, 2, 1, 0).reshape(K, width))

    def synthesis_form(table):
        return to_bf(table.reshape(half, 2, KY, 2).transpose(0, 1, 3, 2).reshape(half, 2 * K))

    return analysis_form(col), synthesis_form(inv), analysis_form(inv), synthesis_form(col)


def blade_tables():
    eye = np.eye(CH)
    spread = np.zeros((4, C, C))
    gather = np.zeros((4, C, C))
    copies = np.zeros((4, C, C))
    unfold = np.zeros((4, C, C))
    for p in range(4):
        for b in range(4):
            q = int(np.where(SELECT[p] == b)[0][0])
            sign = SIGNS[p, q]
            at_p, at_q, at_b = (slice(i * CH, (i + 1) * CH) for i in (p, q, b))
            spread[p, at_q, at_b] = sign * eye
            unfold[p, at_b, at_q] = sign * eye
            gather[p, at_b, at_p] = eye
            copies[p, at_p, at_b] = eye
    return to_bf(spread), to_bf(gather), to_bf(copies), to_bf(unfold)


def mask_table(group):
    row = np.arange(8 * group.own)[:, None]
    lane = np.arange(C)[None, :]
    return (((row % group.own) // (group.own // 4)) == lane // CH).astype(np.float32)


def analysis(block, table):
    stacked = jnp.concatenate([block[:, :C], block[:, C:]], axis=0)
    return dot(table, stacked)


def put_field(field, n, value):
    field[0, pl.ds(pl.multiple_of(n * PITCH, 8), K), :] = value[:, :128]
    field[1, pl.ds(pl.multiple_of(n * PITCH, 8), K), 0:64] = value[:, 128:]


def get_rows(field, k, count):
    low = field[0, pl.ds(k, count, stride=PITCH), :]
    high = field[1, pl.ds(k, count, stride=PITCH), :]
    return jnp.concatenate([low, high[:, :64]], axis=1).astype(BF)


def rows_forward(field, matrix, ky2, count):
    parts = []
    for parity in range(2):
        ky = ky2 * 2 + parity
        parts.append(
            jnp.concatenate([get_rows(field, ky, count), get_rows(field, KY + ky, count)], axis=0)
        )
    return dot(matrix, jnp.concatenate(parts, axis=1))


def rows_inverse(field, matrix_t, spectrum, ky2, count):
    for parity in range(2):
        value = dot(matrix_t, spectrum[:, parity * C : (parity + 1) * C])
        ky = ky2 * 2 + parity
        for part in range(2):
            piece = value[part * count : (part + 1) * count]
            field[0, pl.ds(part * KY + ky, count, stride=PITCH), :] = piece[:, :128]
            field[1, pl.ds(part * KY + ky, count, stride=PITCH), :] = jnp.concatenate(
                [piece[:, 128:], jnp.zeros((count, 64), F32)], axis=1
            )


def synthesis(field, n, table):
    value = jnp.concatenate(
        [field[0, pl.ds(pl.multiple_of(n * PITCH, 8), K), :], field[1, pl.ds(pl.multiple_of(n * PITCH, 8), K), 0:64]], axis=1
    ).astype(BF)
    zero = jnp.zeros((K, C), BF)
    both = jnp.concatenate(
        [jnp.concatenate([value, zero], axis=1), jnp.concatenate([zero, value], axis=1)], axis=0
    )
    return dot(table, both)


def pointwise(block, first, second, product):
    left = product(block[:, :256], first)
    right = product(block[:, 128:], second)
    return jnp.concatenate(
        [left[:, :128], left[:, 128:] + right[:, :128], right[:, 128:]], axis=1
    )


def gelu_and_slope(value):
    cdf = 0.5 + 0.5 * lax.erf(value * (1.0 / math.sqrt(2.0)))
    bell = jnp.exp(-0.5 * value * value)
    return value * cdf, cdf + value * bell * (1.0 / math.sqrt(2.0 * math.pi))


class Group:
    def __init__(self, kind, first, slots, rows, width, parts):
        self.kind, self.first = kind, first
        self.slots, self.rows, self.width = slots, rows, width
        self.count = slots * rows
        self.half = width // 2
        self.block = 1024 // self.half
        self.steps = self.count // self.block
        self.own = 4 * slots * 2
        self.lines = 8 * self.own
        self.stack = max(1, 16 // self.own)
        self.dtype = F32 if self.own % 16 else BF


def struct(shape, dtype=BF):
    return jax.ShapeDtypeStruct(shape, dtype)


def loop(first, last, body, unroll=1):
    def step(i, carry):
        body(i)
        return carry

    lax.fori_loop(first, last, step, 0, unroll=unroll)


STEP = 16


def pack(source, target, group, live=None):
    rows = slice(group.first, group.first + group.count)
    for first in range(0, group.half, STEP):
        slabs = []
        for j in range(first, first + STEP):
            slab = source[rows, j * PAIR : (j + 1) * PAIR]
            slabs.append(slab if live is None else slab * live)
        target[rows, first : first + STEP, :] = jnp.swapaxes(jnp.stack(slabs, axis=0), 0, 1)


def block_of(ref, group, i):
    rows = pl.ds(group.first + i * group.block, group.block)
    return ref[rows].reshape(group.block * group.half, PAIR)


def set_block(ref, group, i, value):
    rows = pl.ds(group.first + i * group.block, group.block)
    ref[rows] = value.reshape(group.block, group.half, PAIR)


def analyse(value, table, field, group, i):
    t = table[...]
    for q in range(group.block):
        put_field(
            field, i * group.block + q, analysis(value[q * group.half : (q + 1) * group.half], t)
        )


def synthesise(field, table, group, i):
    return jnp.concatenate(
        [synthesis(field, i * group.block + q, table[...]) for q in range(group.block)], axis=0
    )


def send_rows(field, matrix, out, group):
    def body(k):
        values = [
            rows_forward(field, matrix[...], k * group.stack + j, group.count)
            for j in range(group.stack)
        ]
        rows = pl.ds(pl.multiple_of(k * 16, 16), 16)
        for owner in range(4):
            block = slice(owner * group.own, (owner + 1) * group.own)
            piece = jnp.concatenate([v[block] for v in values], axis=0)
            out[owner % 2, owner // 2, rows, :] = piece.astype(BF)

    count = 8 // group.stack
    loop(0, count, body, unroll=count)


def receive_rows(field, matrix_t, spectrum, group):
    def body(k):
        rows = pl.ds(pl.multiple_of(k * 16, 16), 16)
        pieces = [spectrum[owner, rows, :] for owner in range(4)]
        if group.stack > 1:
            pieces = [p.astype(F32) for p in pieces]
        for j in range(group.stack):
            block = slice(j * group.own, (j + 1) * group.own)
            value = jnp.concatenate([p[block] for p in pieces], axis=0).astype(BF)
            rows_inverse(field, matrix_t[...], value, k * group.stack + j, group.count)

    count = 8 // group.stack
    loop(0, count, body, unroll=count)


def build_weights(raw, w2):
    def body(ky):
        parts = [jnp.concatenate([raw[m, ky, b] for m in range(4)], axis=0) for b in range(4)]
        w2[ky] = jnp.concatenate(parts, axis=1)

    loop(0, KY, body, unroll=4)


def build_point(point, first, second):
    rows = []
    for p in range(4):
        pieces = []
        for q in range(4):
            piece = point[int(SELECT[p, q])]
            pieces.append(piece if SIGNS[p, q] > 0 else -piece)
        rows.append(jnp.concatenate(pieces, axis=1))
    matrix = jnp.concatenate(rows, axis=0)
    zero = jnp.zeros((C, C), BF)
    both = jnp.concatenate(
        [jnp.concatenate([matrix, zero], axis=1), jnp.concatenate([zero, matrix], axis=1)], axis=0
    )
    first[...] = both[:256, :256]
    second[...] = both[128:, 128:]
    second[0:128, 0:128] = jnp.zeros((128, 128), BF)


def build_rows(modes, table, table_t, place, matrix, matrix_t, group):
    size = KX * group.slots * 2
    per = group.slots * 2
    row = lax.broadcasted_iota(jnp.int32, (size, size), 0)
    lane = lax.broadcasted_iota(jnp.int32, (size, size), 1)
    wanted = jnp.zeros((size, size), jnp.int32)
    for m in range(KX):
        inside = jnp.logical_and(row >= m * per, row < (m + 1) * per)
        wanted = jnp.where(inside, modes[m] * per + row - m * per, wanted)
    chosen = (wanted == lane).astype(F32).astype(BF)
    matrix[...] = dot(chosen, table[place]).astype(BF)
    matrix_t[...] = dot_nt(table_t[place], chosen).astype(BF)


def spread_rows(value, table, out, group, mask=None):
    for parity in range(2):
        part = value[:, parity * C : (parity + 1) * C]
        for p in range(4):
            result = dot(part, table[p])
            if mask is not None:
                result = result * mask[...]
            out[parity, p] = result.astype(group.dtype)


def fold_rows(parts, table, out, index):
    halves = []
    for parity in range(2):
        total = None
        for p in range(4):
            term = dot(parts[parity, p].astype(BF), table[p])
            total = term if total is None else total + term
        halves.append(total)
    out[index] = jnp.concatenate(halves, axis=1).astype(BF)


def ky_rows(parts, parity, ky2, group):
    rows = pl.ds(pl.multiple_of(ky2 * group.own, group.own), group.own)
    return jnp.concatenate([parts[parity, p, rows, :] for p in range(4)], axis=0).astype(BF)


def set_ky_rows(parts, parity, ky2, group, value):
    rows = pl.ds(pl.multiple_of(ky2 * group.own, group.own), group.own)
    for p in range(4):
        parts[parity, p, rows, :] = value[p * group.own : (p + 1) * group.own].astype(group.dtype)


def spectral_forward(x, w2, spread, gather, mask, l, z, out, index, group):
    spread_rows(x, spread, l, group)

    def body(ky2):
        for parity in range(2):
            value = dot_nt(ky_rows(l, parity, ky2, group), w2[ky2 * 2 + parity])
            set_ky_rows(z, parity, ky2, group, value * mask[0 : 4 * group.own, :])

    loop(0, KY // 2, body, unroll=8)
    fold_rows(z, gather, out, index)


def spectral_backward(d, w2, copies, unfold, mask, a, z, out, index, group):
    spread_rows(d, copies, a, group, mask)

    def body(ky2):
        for parity in range(2):
            value = dot(ky_rows(a, parity, ky2, group), w2[ky2 * 2 + parity])
            set_ky_rows(z, parity, ky2, group, value)

    loop(0, KY // 2, body, unroll=8)
    fold_rows(z, unfold, out, index)


def weight_gradient(x, d, spread, copies, mask):
    halves = []
    for parity in range(2):
        lanes = slice(parity * C, (parity + 1) * C)
        total = None
        for p in range(4):
            right = dot(x[:, lanes], spread[p]).astype(BF)
            left = (dot(d[:, lanes], copies[p]) * mask[...]).astype(BF)
            term = dot_tn(left, right)
            total = term if total is None else total + term
        halves.append(total)
    return jnp.concatenate(halves, axis=1)


def point_sums(ds, a, sums, bias_sum):
    sums[0] += dot_tn(ds[:, :256], a[:, :256])
    sums[1] += dot_tn(ds[:, 128:], a[:, 128:])
    bias_sum[...] += jnp.sum(ds.astype(F32).reshape(-1, 8, PAIR), axis=0)


def fold_point(sums, bias_sum, out):
    total = sums[0][:C, :C] + sums[1][64:, 64:]
    grad = None
    for p in range(4):
        row = total[p * CH : (p + 1) * CH]
        pieces = []
        for b in range(4):
            q = int(np.where(SELECT[p] == b)[0][0])
            piece = row[:, q * CH : (q + 1) * CH]
            pieces.append(piece if SIGNS[p, q] > 0 else -piece)
        term = jnp.concatenate(pieces, axis=1)
        grad = term if grad is None else grad + term
    bias = bias_sum[...]
    bias = jnp.sum(bias[:, :C] + bias[:, C:], axis=0, keepdims=True)
    first = lax.broadcasted_iota(jnp.int32, (16, C), 0) == 0
    for k in range(3):
        out[k, :, 0:C] = grad[k * 16 : (k + 1) * 16]
    out[3, :, 0:C] = jnp.where(first, jnp.broadcast_to(bias, (16, C)), 0.0)


class Refs:
    pass


def main_kernel(names, groups, ranks, *refs):
    r = Refs()
    for name, ref in zip(names, refs, strict=True):
        setattr(r, name, ref)
    reduce_here = ranks == 8
    me = lax.axis_index("modes")
    rank = lax.axis_index("dp")
    core = lax.rem(me, 2)
    chip = me // 2
    mate = (rank, chip * 2 + 1 - core)
    across = (rank, lax.rem(me + 2, 4))

    def mode_device(d):
        return (rank, lax.rem(me + d, 4))

    def rank_device(d):
        return (lax.rem(rank + d, ranks), me)

    def local_copy(source, target, sem):
        copy = pltpu.make_async_copy(source, target, sem)
        copy.start()
        return copy

    def remote(source, target, send, recv, device):
        copy = pltpu.make_async_remote_copy(
            src_ref=source,
            dst_ref=target,
            send_sem=send,
            recv_sem=recv,
            device_id=device,
            device_id_type=pl.DeviceIdType.MESH,
        )
        copy.start()
        return copy

    def per_kind(name):
        return [getattr(r, f"{name}{g.kind}") for g in groups]

    def per_group(name):
        return [getattr(r, f"{name}{g}") for g in range(len(groups))]

    a0, a1, slope, grad, delta = [per_kind(n) for n in ("a0", "a1", "sl", "g", "d")]
    stage, mask, matrix, matrix_t = [per_kind(n) for n in ("stage", "mask", "m", "mt")]
    outs, backs, l, z = [per_kind(n) for n in ("out", "back", "l", "z")]
    tables = [[getattr(r, f"t{g.kind}{k}") for k in range(4)] for g in groups]
    field, send, recv, out_x, in_x, full = [
        per_group(n) for n in ("field", "send", "recv", "outx", "inx", "full")
    ]
    points = [(r.pa1, r.pb1), (r.pa2, r.pb2)]
    B1, B2, S1, S2 = range(4)

    loads = [
        local_copy(r.grids1, r.stage1, r.in_sem.at[1]),
        local_copy(r.grids0, r.stage0, r.in_sem.at[0]),
    ][::-1]
    raw_load = local_copy(r.spec1, r.raw, r.in_sem.at[2])

    barrier = pltpu.get_barrier_semaphore()
    for d in range(1, 4):
        pl.semaphore_signal(barrier, inc=1, device_id=mode_device(d), device_id_type=pl.DeviceIdType.MESH)
    if reduce_here:
        for d in range(1, ranks):
            pl.semaphore_signal(barrier, inc=1, device_id=rank_device(d), device_id_type=pl.DeviceIdType.MESH)

    for kind in (1, 0):
        group = groups[2 * kind]
        build_rows(
            r.modes, getattr(r, f"rt{kind}"), getattr(r, f"rtt{kind}"), me,
            getattr(r, f"m{kind}"), getattr(r, f"mt{kind}"), group,
        )
    pl.semaphore_wait(barrier, 3 + (ranks - 1 if reduce_here else 0))

    flights = [{} for _ in groups]

    def hop(g, k, source, target, device):
        flights[g][k] = remote(source, target, r.hops.at[g, k, 0], r.hops.at[g, k, 1], device)

    def start(g):
        send_rows(field[g], matrix[g], send[g], groups[g])
        hop(g, 0, send[g].at[1 - core], recv[g], mate)

    def cross(g):
        if 0 not in flights[g]:
            return
        flights[g].pop(0).wait()
        total = send[g][core, 1 - chip].astype(F32) + recv[g][1 - chip].astype(F32)
        out_x[g][...] = total.astype(BF)
        hop(g, 1, out_x[g], in_x[g], across)

    def land(g, spectral, layer):
        if 1 not in flights[g]:
            return
        flights[g].pop(1).wait()
        total = send[g][core, chip].astype(F32) + recv[g][chip].astype(F32)
        total = total + in_x[g][...].astype(F32)
        spectral(g, layer, total)
        hop(g, 2, full[g].at[me], full[g].at[me], across)
        hop(g, 3, full[g].at[me], full[g].at[me], mate)

    def forward(g):
        if 2 not in flights[g]:
            return
        flights[g].pop(2).wait()
        slot = lax.rem(me + 2, 4)
        hop(g, 4, full[g].at[slot], full[g].at[slot], mate)

    def arrive(g):
        flights[g].pop(3).wait()
        flights[g].pop(4).wait()
        receive_rows(field[g], matrix_t[g], full[g], groups[g])

    def keep(g, layer, which, total):
        group = groups[g]
        rows = slice(group.keep, group.keep + group.own)
        r.factors[layer, which, :, rows, :] = total.reshape(8, group.own, PAIR).astype(BF)

    def spectral(g, layer, total):
        keep(g, layer, 0, total)
        w2 = (r.w21, r.w22)[layer]
        spectral_forward(
            total.astype(BF), w2, r.spread, r.gather, mask[g], l[g], z[g], full[g], me, groups[g]
        )

    def spectral_back(g, layer, total):
        keep(g, layer, 1, total)
        w2 = (r.w21, r.w22)[layer]
        spectral_backward(
            total.astype(BF), w2, r.copies, r.unfold, mask[g], l[g], z[g], full[g], me, groups[g]
        )

    writes = []
    factor_copies = {}

    def start_factors(layer, which):
        if not reduce_here:
            return
        factor_copies[layer, which] = [
            remote(
                r.factors.at[layer, which, lax.rem(rank + d, ranks)],
                r.factors_in.at[layer, which, d],
                r.dw_send.at[layer, which, d - 1],
                r.dw_recv.at[layer, which, d - 1],
                rank_device(d),
            )
            for d in range(1, ranks)
        ]

    def end_factors(layer):
        target = (r.spec_out1, r.spec_out2)[layer]
        if not reduce_here:
            mask_rows = r.keep_mask[...]

            def body(ky2):
                r.dws[ky2] = weight_gradient(
                    r.factors[layer, 0, ky2], r.factors[layer, 1, ky2], r.spread, r.copies, mask_rows
                ).astype(BF)

            loop(0, 8, body)
            copy = local_copy(r.dws, target, r.out_sem.at[layer])
            copy.wait()
            return
        values = []
        for which in range(2):
            for copy in factor_copies[layer, which]:
                copy.wait()
            pieces = [r.factors[layer, which, rank]]
            pieces += [r.factors_in[layer, which, d] for d in range(1, ranks)]
            values.append(jnp.concatenate(pieces, axis=0))
        mask_rows = jnp.concatenate([r.keep_mask[...]] * ranks, axis=0)
        r.dws[layer] = weight_gradient(*values, r.spread, r.copies, mask_rows)
        writes.append(local_copy(r.dws.at[layer], target, r.out_sem.at[layer]))

    point_copies = {}

    def point_first(layer):
        fold_point(r.sums.at[layer], r.bias_sum.at[layer], r.pt_send.at[layer])
        if reduce_here:
            point_copies[layer] = [
                remote(
                    r.pt_send.at[layer, lax.rem(me + d, 4)],
                    r.pt_one.at[layer, d - 1],
                    r.pt_sems.at[layer, 0, d - 1],
                    r.pt_sems.at[layer, 1, d - 1],
                    mode_device(d),
                )
                for d in range(1, 4)
            ]

    def point_second(layer):
        if not reduce_here:
            return
        for copy in point_copies[layer]:
            copy.wait()
        total = r.pt_send[layer, me]
        for d in range(3):
            total = total + r.pt_one[layer, d]
        r.pt_two[layer, rank] = total
        point_copies[layer] = [
            remote(
                r.pt_two.at[layer, rank],
                r.pt_two.at[layer, rank],
                r.pt_sems.at[layer, 2, d - 1],
                r.pt_sems.at[layer, 3, d - 1],
                rank_device(d),
            )
            for d in range(1, ranks)
        ]

    def point_third(layer):
        if not reduce_here:
            return
        for copy in point_copies[layer]:
            copy.wait()
        total = r.pt_two[layer, 0]
        for k in range(1, ranks):
            total = total + r.pt_two[layer, k]
        r.pt_full[layer, me] = total
        point_copies[layer] = [
            remote(
                r.pt_full.at[layer, me],
                r.pt_full.at[layer, me],
                r.pt_sems.at[layer, 4, d - 1],
                r.pt_sems.at[layer, 5, d - 1],
                mode_device(d),
            )
            for d in range(1, 4)
        ]

    def point_last(layer):
        source = r.pt_full if reduce_here else r.pt_send
        if reduce_here:
            for copy in point_copies[layer]:
                copy.wait()
        target = (r.point_out1, r.point_out2)[layer]
        writes.append(local_copy(source.at[layer], target, r.out_sem.at[2 + layer]))

    def first(g):
        group = groups[g]
        pack(stage[g], a0[g], group)

        def body(i):
            analyse(block_of(a0[g], group, i), tables[g][0], field[g], group, i)

        loop(0, group.steps, body)

    def pack_grad(g):
        group = groups[g]
        slot = lax.broadcasted_iota(jnp.int32, (group.count, PAIR), 0) // group.rows
        slot = slot + group.first // group.rows
        count = (r.count0, r.count1)[group.kind][0]
        pack(stage[g], grad[g], group, (slot < count).astype(F32).astype(BF))

    def before_gelu(g, i, x, layer):
        first, second = points[layer]
        linear = pointwise(x, first[...], second[...], dot_nt)
        return synthesise(field[g], tables[g][1], groups[g], i) + linear + r.bias_pair[layer]

    def middle(g, i):
        group = groups[g]
        x = block_of(a0[g], group, i)
        gelu, sl = gelu_and_slope(before_gelu(g, i, x, 0))
        value = (x.astype(F32) + gelu).astype(BF)
        set_block(a1[g], group, i, value)
        set_block(slope[g], group, i, sl.astype(BF))
        analyse(value, tables[g][0], field[g], group, i)

    def turn(g, i):
        group = groups[g]
        x = block_of(a1[g], group, i)
        gelu, sl = gelu_and_slope(before_gelu(g, i, x, 1))
        d = (block_of(grad[g], group, i).astype(F32) * sl).astype(BF)
        set_block(a1[g], group, i, (x.astype(F32) + gelu).astype(BF))
        set_block(delta[g], group, i, d)
        point_sums(d, x, r.sums.at[1], r.bias_sum.at[1])
        analyse(d, tables[g][2], field[g], group, i)

    def gradient(g, i, layer):
        group = groups[g]
        first, second = points[layer]
        linear = pointwise(block_of(delta[g], group, i), first[...], second[...], dot)
        spectral_part = synthesise(field[g], tables[g][3], group, i)
        return spectral_part + linear + block_of(grad[g], group, i).astype(F32)

    def back(g, i):
        group = groups[g]
        g1 = gradient(g, i, 1)
        set_block(grad[g], group, i, g1.astype(BF))
        d = (g1 * block_of(slope[g], group, i).astype(F32)).astype(BF)
        set_block(delta[g], group, i, d)
        point_sums(d, block_of(a0[g], group, i), r.sums.at[0], r.bias_sum.at[0])
        analyse(d, tables[g][2], field[g], group, i)

    def final(g, i):
        set_block(grad[g], groups[g], i, gradient(g, i, 0).astype(BF))

    def write_rows(g, sources, targets, sem):
        rows = pl.ds(groups[g].first, groups[g].count)
        writes.append(local_copy(sources[g].at[rows], targets[g].at[rows], r.row_sem.at[sem, g]))

    def period(step, previous, layer, following, next_layer, after_all=None, each=None):
        def done(g):
            if each is not None:
                each(g)
            start(g)

        arrive(S1)
        forward(B1)
        step(S1, 0)
        cross(B2)
        done(S1)
        land(S2, previous, layer)
        arrive(B1)
        cross(S1)
        step(B1, 0)
        land(B2, previous, layer)
        if after_all is not None:
            after_all()
        step(B1, 1)
        forward(S2)
        done(B1)
        land(S1, following, next_layer)
        arrive(S2)
        cross(B1)
        forward(B2)
        step(S2, 0)
        done(S2)
        arrive(B2)
        step(B2, 0)
        cross(S2)
        land(B1, following, next_layer)
        forward(S1)
        step(B2, 1)
        done(B2)

    loads[1].wait()
    first(S1)
    start(S1)
    loads[0].wait()
    first(B1)
    cross(S1)
    start(B1)
    first(S2)
    cross(B1)
    start(S2)
    first(B2)
    cross(S2)
    start(B2)
    loads = [local_copy(r.cot0, r.stage0, r.in_sem.at[0]), local_copy(r.cot1, r.stage1, r.in_sem.at[1])]
    raw_load.wait()
    build_weights(r.raw, r.w21)
    raw_load = local_copy(r.spec2, r.raw, r.in_sem.at[2])
    land(S1, spectral, 0)
    cross(B2)
    land(B1, spectral, 0)
    for k, value in enumerate((r.bias1, r.bias2)):
        row = value[...].reshape(1, C)
        r.bias_pair[k] = jnp.concatenate([row, row], axis=1)
    build_point(r.point1, *points[0])
    build_point(r.point2, *points[1])
    r.sums[...] = jnp.zeros_like(r.sums)
    r.bias_sum[...] = jnp.zeros_like(r.bias_sum)
    r.pt_send[...] = jnp.zeros_like(r.pt_send)
    land(S2, spectral, 0)
    loads[1].wait()
    pack_grad(S1)
    pack_grad(S2)
    forward(S1)
    land(B2, spectral, 0)
    loads[0].wait()
    pack_grad(B1)
    forward(B1)
    pack_grad(B2)
    raw_load.wait()
    build_weights(r.raw, r.w22)

    start_factors(0, 0)

    period(middle, spectral, 0, spectral, 1)
    period(
        turn, spectral, 1, spectral_back, 1,
        after_all=lambda: start_factors(1, 0),
        each=lambda g: write_rows(g, a1, outs, 0),
    )
    point_first(1)
    period(
        back, spectral_back, 1, spectral_back, 0,
        after_all=lambda: (point_second(1), start_factors(1, 1)),
    )
    point_first(0)

    def finish_rows(g):
        for i in range(groups[g].steps):
            final(g, i)
        write_rows(g, grad, backs, 1)

    arrive(S1)
    forward(B1)
    finish_rows(S1)
    cross(B2)
    point_third(1)
    point_second(0)
    land(S2, spectral_back, 0)
    arrive(B1)
    end_factors(1)
    land(B2, spectral_back, 0)
    start_factors(0, 1)
    finish_rows(B1)
    forward(S2)
    forward(B2)
    point_last(1)
    point_third(0)
    arrive(S2)
    finish_rows(S2)
    end_factors(0)
    arrive(B2)
    finish_rows(B2)
    point_last(0)
    for copy in writes:
        copy.wait()


def finish_kernel(*refs, groups, reduce_here):
    refs = list(refs)
    counts = [refs.pop(0) for _ in groups]
    sources = [(refs.pop(0), refs.pop(0)) for _ in groups]
    if reduce_here:
        layers_in = [(refs.pop(0), refs.pop(0)) for _ in range(2)]
    targets = [(refs.pop(0), refs.pop(0)) for _ in groups]
    if reduce_here:
        layers_out = [(refs.pop(0), refs.pop(0), refs.pop(0)) for _ in range(2)]
        lines, flat = refs
    step = pl.program_id(0)
    for group, count, (out_in, back_in), (out, back) in zip(groups, counts, sources, targets):
        row = lax.broadcasted_iota(jnp.int32, (16, PAIR), 0) + step * 16
        live = (row // group.rows < count[0]).astype(F32).astype(BF)
        for source, target, factor in ((out_in, out, live), (back_in, back, None)):
            for first in range(0, group.half, STEP):
                value = jnp.swapaxes(source[:, first : first + STEP, :], 0, 1)
                for j in range(STEP):
                    slab = value[j] if factor is None else value[j] * factor
                    lane = (first + j) * PAIR
                    target[:, lane : lane + PAIR] = slab
    if not reduce_here:
        return
    for k, ((spec_in, point_in), (spec, point, bias)) in enumerate(zip(layers_in, layers_out)):

        @pl.when(step == k)
        def _(spec_in=spec_in, point_in=point_in, spec=spec, point=point, bias=bias):
            for t in range(3):
                lines[t, 0:C, :] = spec_in[:, t * 128 : (t + 1) * 128]
            rows = [
                jnp.concatenate([lines[t, pl.ds(o, 24, stride=8), :] for t in range(3)], axis=1)
                for o in range(8)
            ]
            for block in range(8):
                lane = block * CH
                value = jnp.concatenate([v[:, lane : lane + CH] for v in rows], axis=1)
                for t in range(3):
                    flat[t, pl.ds(block * 24, 24), :] = value[:, t * 128 : (t + 1) * 128]
            for block in range(8):
                for high in range(6):
                    for t in range(3):
                        lane = (block * 6 + high) * PAIR + t * 128
                        spec[:, lane : lane + 128] = flat[t, pl.ds(block * 24 + high, 4, stride=6), :]
            for b in range(4):
                for q in range(3):
                    point[b, q * 16 : (q + 1) * 16, :] = point_in[q][:, b * CH : (b + 1) * CH]
            bias[...] = point_in[3][0:1, :C]


def finish(counts, outs, backs, layers, groups, reduce_here):
    def whole(shape):
        return pl.BlockSpec(shape, lambda i: (0,) * len(shape))

    operands, in_specs = list(counts), [pl.BlockSpec(memory_space=pltpu.SMEM)] * len(groups)
    out_specs, out_shape, scratch = [], [], []
    for group, out, back in zip(groups, outs, backs):
        operands += [out, back]
        in_specs += [pl.BlockSpec((16, group.half, PAIR), lambda i: (i, 0, 0))] * 2
        out_specs += [pl.BlockSpec((16, group.width * C), lambda i: (i, 0))] * 2
        out_shape += [struct((group.count, group.width * C))] * 2
    if reduce_here:
        for spec, point in layers:
            operands += [spec, point]
            in_specs += [whole(spec.shape), whole(point.shape)]
            shapes = [(4, C * PAIR // 4), (4, CH, CH), (1, C)]
            out_specs += [whole(s) for s in shapes]
            out_shape += [struct(s, F32) for s in shapes]
        scratch = [pltpu.VMEM((3, C + 64, 128), F32)] * 2
    return pl.pallas_call(
        lambda *refs: finish_kernel(*refs, groups=groups, reduce_here=reduce_here),
        grid=(groups[0].count // 16,),
        in_specs=in_specs,
        out_specs=out_specs,
        out_shape=out_shape,
        scratch_shapes=scratch,
        compiler_params=pltpu.CompilerParams(vmem_limit_bytes=LIMIT),
    )(*operands)


def row_tables(group, parts):
    height = group.rows * parts
    frequency = np.arange(KX)
    frequency = np.where(frequency < KX // 2, frequency, frequency - KX)
    phase = (frequency[:, None] * np.arange(height)[None, :]) % height
    phase = phase.astype(np.float32) * np.float32(2.0 * math.pi / height)
    cosine, sine = np.cos(phase), np.sin(phase)
    both = np.stack([np.stack([cosine, sine], 1), np.stack([-sine, cosine], 1)], 1)
    both = both.reshape(KX, 2, 2, parts, group.rows)
    full = np.zeros((parts, KX, group.slots, 2, 2, group.slots, group.rows), np.float32)
    for s in range(group.slots):
        full[:, :, s, :, :, s, :] = both.transpose(3, 0, 1, 2, 4)
    full = full.reshape(parts, KX * group.slots * 2, 2 * group.count)
    return to_bf(full), to_bf(full.transpose(0, 2, 1))


def local(
    grids_big,
    grids_small,
    counts_big,
    counts_small,
    mode_table,
    spec_one,
    point_one,
    bias_one,
    spec_two,
    point_two,
    bias_two,
    cot_big,
    cot_small,
):
    parts = lax.axis_size("modes")
    ranks = lax.axis_size("dp")
    reduce_here = ranks == 8
    kinds, groups = [], []
    for kind, grids in enumerate((grids_big, grids_small)):
        slots, rows, width = grids.shape[0], grids.shape[1], grids.shape[2] // C
        kinds.append(Group(kind, 0, slots, rows, width, parts))
        for part in range(2):
            groups.append(Group(kind, part * slots * rows // 2, slots // 2, rows, width, parts))
    total_rows = 0
    for group in groups[2:] + groups[:2]:
        group.keep = total_rows
        total_rows += group.own
    inputs, outputs, scratch = {}, {}, {}
    smem, vmem, hbm = pltpu.SMEM, pltpu.VMEM, pl.ANY
    inputs["count0"] = (counts_big, smem)
    inputs["count1"] = (counts_small, smem)
    inputs["modes"] = (mode_table, smem)
    arrays = ((grids_big, cot_big), (grids_small, cot_small))
    spread, gather, copies, unfold = blade_tables()
    for k, kind in enumerate(kinds):
        group = groups[2 * k]
        flat = (kind.count, kind.width * C)
        inputs[f"grids{k}"] = (arrays[k][0].reshape(flat), hbm)
        inputs[f"cot{k}"] = (arrays[k][1].reshape(flat), hbm)
        for t, table in enumerate(column_tables(kind.rows * parts, kind.width)):
            inputs[f"t{k}{t}"] = (jnp.asarray(table), vmem)
        straight, turned = row_tables(group, parts)
        inputs[f"rt{k}"] = (jnp.asarray(straight), vmem)
        inputs[f"rtt{k}"] = (jnp.asarray(turned), vmem)
        inputs[f"mask{k}"] = (jnp.asarray(mask_table(group)), vmem)
        scratch[f"m{k}"] = pltpu.VMEM(straight.shape[1:], BF)
        scratch[f"mt{k}"] = pltpu.VMEM(turned.shape[1:], BF)
        rows = (kind.count, kind.half, PAIR)
        outputs[f"out{k}"] = struct(rows)
        outputs[f"back{k}"] = struct(rows)
        scratch[f"stage{k}"] = pltpu.VMEM(flat, BF)
        for name in ("a0", "a1", "sl", "g", "d"):
            scratch[f"{name}{k}"] = pltpu.VMEM(rows, BF)
        for name in ("l", "z"):
            scratch[f"{name}{k}"] = pltpu.VMEM((2, 4, group.lines, C), group.dtype)
    for g, group in enumerate(groups):
        lines = (group.lines, PAIR)
        scratch[f"field{g}"] = pltpu.VMEM((2, group.count * PITCH + PITCH, 128), F32)
        scratch[f"send{g}"] = pltpu.VMEM((2, 2, *lines), BF)
        scratch[f"recv{g}"] = pltpu.VMEM((2, *lines), BF)
        scratch[f"full{g}"] = pltpu.VMEM((4, *lines), BF)
        for name in ("outx", "inx"):
            scratch[f"{name}{g}"] = pltpu.VMEM(lines, BF)
    for name, table in (("spread", spread), ("gather", gather), ("copies", copies), ("unfold", unfold)):
        inputs[name] = (jnp.asarray(table), vmem)
    keep_mask = np.concatenate([mask_table(g)[: g.own] for g in groups[2:] + groups[:2]])
    inputs["keep_mask"] = (jnp.asarray(keep_mask), vmem)
    layers = ((point_one, bias_one, spec_one), (point_two, bias_two, spec_two))
    for k, (point, bias, spec) in enumerate(layers, 1):
        inputs[f"point{k}"] = (point, vmem)
        inputs[f"bias{k}"] = (bias, vmem)
        inputs[f"spec{k}"] = (spec, hbm)
        outputs[f"spec_out{k}"] = struct((C, PAIR), F32) if reduce_here else struct((8, C, PAIR))
        outputs[f"point_out{k}"] = struct((4, 16, 256), F32)
        scratch[f"pa{k}"] = pltpu.VMEM((256, 256), BF)
        scratch[f"pb{k}"] = pltpu.VMEM((256, 256), BF)
        scratch[f"w2{k}"] = pltpu.VMEM((KY, C, C), BF)
    scratch["raw"] = pltpu.VMEM(spec_one.shape, BF)
    scratch["bias_pair"] = pltpu.VMEM((2, 1, PAIR), F32)
    scratch["sums"] = pltpu.VMEM((2, 2, 256, 256), F32)
    scratch["bias_sum"] = pltpu.VMEM((2, 8, PAIR), F32)
    scratch["pt_send"] = pltpu.VMEM((2, 4, 16, 256), F32)
    dma = pltpu.SemaphoreType.DMA
    if reduce_here:
        scratch["factors_in"] = pltpu.VMEM((2, 2, ranks, total_rows, PAIR), BF)
        scratch["dws"] = pltpu.VMEM((2, C, PAIR), F32)
        scratch["pt_one"] = pltpu.VMEM((2, 3, 16, 256), F32)
        scratch["pt_two"] = pltpu.VMEM((2, ranks, 16, 256), F32)
        scratch["pt_full"] = pltpu.VMEM((2, 4, 16, 256), F32)
        scratch["dw_send"] = dma((2, 2, ranks - 1))
        scratch["dw_recv"] = dma((2, 2, ranks - 1))
        scratch["pt_sems"] = dma((2, 6, ranks - 1))
    else:
        scratch["dws"] = pltpu.VMEM((8, C, PAIR), BF)
    scratch["factors"] = pltpu.VMEM((2, 2, 8, total_rows, PAIR), BF)
    scratch["hops"] = dma((4, 5, 2))
    scratch["in_sem"] = dma((3,))
    scratch["out_sem"] = dma((4,))
    scratch["row_sem"] = dma((2, 4))
    names = list(inputs) + list(outputs) + list(scratch)
    result = pl.pallas_call(
        lambda *refs: main_kernel(names, groups, ranks, *refs),
        in_specs=[pl.BlockSpec(memory_space=space) for _, space in inputs.values()],
        out_specs=[pl.BlockSpec(memory_space=hbm)] * len(outputs),
        out_shape=list(outputs.values()),
        scratch_shapes=list(scratch.values()),
        compiler_params=pltpu.CompilerParams(
            vmem_limit_bytes=LIMIT, collective_id=0, has_side_effects=True
        ),
    )(*[value for value, _ in inputs.values()])
    result = dict(zip(outputs, result))
    layers = [(result[f"spec_out{k}"], result[f"point_out{k}"]) for k in (1, 2)]
    final = finish(
        (counts_big, counts_small),
        (result["out0"], result["out1"]),
        (result["back0"], result["back1"]),
        layers, kinds, reduce_here,
    )
    out_big, back_big, out_small, back_small = [
        v.reshape(k.slots, k.rows, k.width * C) for v, k in zip(final, (kinds[0],) * 2 + (kinds[1],) * 2)
    ]
    if reduce_here:
        grads = [v.reshape(C) if v.shape == (1, C) else v for v in final[4:]]
        return (out_big, out_small, back_big, back_small, *grads)

    grads = []
    for spec, point in layers:
        spec = spec.reshape(8, 4, CH, 2, 4, CH).transpose(0, 3, 4, 1, 2, 5)
        spec = spec.reshape(ranks, 64 // ranks, 4, CH, CH).astype(F32)
        spec = lax.psum_scatter(spec, "dp", scatter_dimension=0, tiled=False)
        point = lax.psum(point, ("dp", "modes")).reshape(64, 256)
        weight = point[:CH, :C].reshape(CH, 4, CH).transpose(1, 0, 2)
        grads += [spec.transpose(1, 0, 2, 3).reshape(4, -1), weight, point[CH, :C]]
    return (out_big, out_small, back_big, back_small, *grads)


def solution(mesh):
    rows = P("dp", "modes", None)
    spec = P("modes", None, None, None, None)
    return jax.shard_map(
        local,
        mesh=mesh,
        in_specs=(rows, rows, P("dp"), P("dp"), P(), spec, P(), P(), spec, P(), P(), rows, rows),
        out_specs=(rows, rows, rows, rows, P("modes", "dp"), P(), P(), P("modes", "dp"), P(), P()),
        check_vma=False,
    )
```
